256 devices in a mesh: tile: 8 (over z_lo, y), epoch: 32 (over x, z_hi, core).
Axes of the slice: x: 4, y: 4, z: 8 (z_hi: 4, z_lo: 2; z = z_hi * 2 + z_lo), core: 2. Of those that a mesh axis runs over, the one named last changes fastest.
Arguments:
- scene: float32 [2, 256, 1024], P(None, 'epoch', 'tile'), may hold values from -6 to 6
- kernels_h: float32 [64, 2, 5, 21], P('epoch'), may hold values from -1.25 to 1.25
- kernels_v: float32 [64, 2, 5, 21], P('epoch'), may hold values from -1.25 to 1.25
- coeffs: bfloat16 [64, 5, 256, 1024], P('epoch', None, None, 'tile'), may hold values from -2.5 to 2.5
- observed: bfloat16 [64, 2, 256, 1024], P('epoch', None, None, 'tile'), may hold values from -6 to 6
- good_pixels: int32 [64, 256, 1024], P('epoch', None, 'tile'), may hold values 0 or 1
- coverage: int32 [64, 8], P('epoch', 'tile'), may hold values 0 or 1
- offsets: int32 [64, 8, 2], P('epoch', 'tile'), may hold values from -8 to 8, as said below
Outputs:
- scene_grad: float32 [2, 256, 1024], P(None, 'epoch', 'tile')
The draws below stay inside these ranges and needn't reach their ends.
Inputs may be any that keep to these rules, and one draw needn't show every extreme that they name: offsets[e, t] = (dy, dx); every offset lies in the stated range, and both ends of it are reached in each draw.
All inputs are finite; a program needn't handle non-finite values. No bound on the sum of `good_pixels` or of `coverage` on one device may be relied on, other than what follows from the above.
Results may differ from the reference program's by a relative error of at most 0.0003.
Values sent between devices are 32-bit elements; how exact they have to be, the bound alone decides.
A program may use at most 64 MiB of HBM per device.

```python
import jax
import jax.numpy as jnp
from jax import lax

BANDS = 2
NBASIS = 5
TAPS = 21
SHIFT = 8
H = 256
W = 128
TILES = 8
EPOCHS = 64
NW = 1024
N_TILE = 8


def draw_offsets(key, part):
    key = jax.random.fold_in(key, 5)
    values = jax.random.randint(jax.random.fold_in(key, 1), (EPOCHS, TILES, 2), -SHIFT, SHIFT + 1)
    first = jax.random.randint(jax.random.fold_in(key, 2), (), 0, EPOCHS)
    second = jax.random.randint(jax.random.fold_in(key, 3), (), 0, EPOCHS)
    values = values.at[first, 0, 0].set(SHIFT).at[first, 0, 1].set(-SHIFT)
    values = values.at[second, TILES - 1, 0].set(-SHIFT).at[second, TILES - 1, 1].set(SHIFT)
    return values.astype(jnp.int32)


def with_ends(drawn, rng, smallest, top_value):
    index_at = [jax.random.randint(jax.random.fold_in(rng, axis), (), 0, length) for axis, length in enumerate(drawn.shape)]
    main_axis = drawn.shape.index(max(drawn.shape))
    neighbour = index_at[:main_axis] + [(index_at[main_axis] + 1) % drawn.shape[main_axis]] + index_at[main_axis + 1:]
    return drawn.at[tuple(index_at)].set(smallest).at[tuple(neighbour)].set(top_value)


def steps_of(stream_key, extent, split, smallest, top_value):
    factor_of = 1.0
    for dim, shards_of in split:
        heights = jax.random.uniform(jax.random.fold_in(jax.random.fold_in(stream_key, 6), dim), (shards_of,), jnp.float32, smallest / len(split), top_value / len(split))
        factor_of = factor_of * jnp.repeat(jnp.exp(heights), extent[dim] // shards_of).reshape((-1,) + (1,) * (len(extent) - 1 - dim))
    return factor_of


def normal_values(rng, extent, deviation, bound, shards=(), kind=jnp.bfloat16):
    drawn = jax.random.normal(rng, extent, jnp.float32) * deviation
    if len(shards) > 0:
        drawn = steps_of(rng, extent, shards, -0.22, 0.18) * drawn
    return jnp.clip(drawn, min=-bound, max=bound).astype(kind)


def setup_inputs(seed: int = 0) -> dict:
    key_list = jax.random.split(jax.random.key(seed), 9)
    scene = normal_values(key_list[0], (BANDS, H, NW), 1.0, 6.0, ((1, 32), (2, 8)), jnp.float32)
    kernels_h = normal_values(key_list[1], (EPOCHS, BANDS, NBASIS, TAPS), TAPS ** -0.5, 1.25, ((0, 32),), jnp.float32)
    kernels_v = normal_values(key_list[2], (EPOCHS, BANDS, NBASIS, TAPS), TAPS ** -0.5, 1.25, ((0, 32),), jnp.float32)
    coeffs = normal_values(key_list[3], (EPOCHS, NBASIS, H, NW), NBASIS ** -0.5, 2.5, ((0, 32), (3, 8)))
    observed = normal_values(key_list[4], (EPOCHS, BANDS, H, NW), 1.0, 6.0, ((0, 32), (3, 8)))
    good_pixels = with_ends((jax.random.randint(key_list[5], (EPOCHS, H, NW), 0, 10) < 9).astype(jnp.int32), jax.random.fold_in(key_list[5], 1), 0, 1)
    coverage = with_ends((jax.random.randint(key_list[6], (EPOCHS, TILES), 0, 4) < 3).astype(jnp.int32), jax.random.fold_in(key_list[6], 1), 0, 1)
    offsets = draw_offsets(jax.random.fold_in(key_list[8], 71), 0)
    return {"scene": scene, "kernels_h": kernels_h, "kernels_v": kernels_v, "coeffs": coeffs, "observed": observed, "good_pixels": good_pixels, "coverage": coverage, "offsets": offsets}


def predict(window, horiz, vert, maps, reach, rows, width):
    taps = horiz.shape[-1]
    across = horiz[:, :, 0, None, None] * window[:, None, :, 0:width]
    for index in range(1, taps):
        across = across + horiz[:, :, index, None, None] * window[:, None, :, index:index + width]
    down = vert[:, :, 0, None, None] * across[:, :, 0:rows, :]
    for index in range(1, taps):
        down = down + vert[:, :, index, None, None] * across[:, :, index:index + rows, :]
    return lax.optimization_barrier(jnp.sum(down * maps[None], axis=1))

def reference(scene, kernels_h, kernels_v, coeffs, observed, good_pixels, coverage, offsets):
    reach = (TAPS - 1) // 2
    margin = SHIFT + reach
    padded = jnp.pad(scene, ((0, 0), (margin, margin), (margin, margin)))

    def epoch_step(total, items):
        horiz, vert, maps, seen, good, cover, shifts = items
        maps = maps.astype(jnp.float32)

        def model(field):
            blocks = []
            for tile in range(N_TILE):
                start_row = (margin + shifts[tile, 0] - reach).astype(jnp.int32)
                start_col = (margin + tile * W + shifts[tile, 1] - reach).astype(jnp.int32)
                window = lax.dynamic_slice(field, (jnp.int32(0), start_row, start_col), (BANDS, H + 2 * reach, W + 2 * reach))
                blocks.append(predict(window, horiz, vert, maps[:, :, tile * W:(tile + 1) * W], reach, H, W))
            return jnp.concatenate(blocks, axis=2)
        image, pullback = jax.vjp(model, padded)
        weight = (good * jnp.repeat(cover, W)[None, :]).astype(jnp.float32)
        residual = weight[None] * (image - seen.astype(jnp.float32))
        grad, = pullback(residual.astype(image.dtype))
        return (total + grad, None)
    total, unused = lax.scan(epoch_step, jnp.zeros_like(padded), (kernels_h, kernels_v, coeffs, observed, good_pixels, coverage, offsets))
    return total[:, margin:margin + H, margin:margin + W * N_TILE]
```

```python
import functools

import jax
import jax.numpy as jnp
from jax import lax
from jax.experimental import pallas as pl
from jax.experimental.pallas import tpu as pltpu
from jax.sharding import PartitionSpec as P

BANDS, NBASIS, TAPS = 2, 5, 21
LOCAL = 2
ROWS, W, TILES = 256, 128, 8
HALF = 128
REACH = 10
NX, NZ, NC = 4, 4, 2
F32, BF16 = jnp.float32, jnp.bfloat16
MESH = pl.DeviceIdType.MESH


def split2(value):
    hi = value.astype(BF16)
    return hi, (value - hi.astype(F32)).astype(BF16)


def mm(a, b):
    return jnp.dot(a, b, preferred_element_type=F32)


def prepare_taps(taps_in, taps):
    taps[...] = jnp.zeros_like(taps)
    lane = lax.broadcasted_iota(jnp.int32, (NBASIS, W), 1)
    for e in range(LOCAL):
        for b in range(BANDS):
            taps[0, e, b, 0:NBASIS, 0:TAPS] = taps_in[e, b]
            row = taps[0, e, b, 0:NBASIS, :]
            back = jnp.zeros((NBASIS, W), F32)
            for a in range(TAPS):
                back = jnp.where(lane == TAPS - 1 - a, row[:, a : a + 1], back)
            taps[1, e, b, 0:NBASIS, :] = back


def build_bands(lo, hi, offsets, th, tv, hf, hb, vf, vb):
    row = lax.broadcasted_iota(jnp.int32, (W, W), 0)
    lane = lax.broadcasted_iota(jnp.int32, (W, W), 1)
    near = jnp.abs(row - lane) < W // 2

    def circulant(taps, flipped, e, b, k, shift):
        base = jnp.broadcast_to(taps[flipped, e, b, pl.ds(k, 1), :], (8, W))
        for bit in (1, 2, 4):
            base = jnp.where((row[0:8] & bit) != 0, pltpu.roll(base, bit, axis=1), base)
        base = pltpu.roll(base, shift, axis=1)
        full = jnp.concatenate([base] + [pltpu.roll(base, g, axis=1) for g in range(8, W, 8)], axis=0)
        return jnp.where(near, full, 0.0), jnp.where(near, 0.0, full)

    def step(i, carry):
        b, k = i // NBASIS, i % NBASIS
        for e in range(LOCAL):
            dy, dx = offsets[e, 0, 0], offsets[e, 0, 1]
            main, edge = circulant(th, 1, e, b, k, W - REACH - dx)
            for part, (m, s) in enumerate(zip(split2(main), split2(edge))):
                hf[part, b, k, 0:W, e * W : (e + 1) * W] = m
                hf[part, b, k, W : 2 * W, e * W : (e + 1) * W] = s
            main, edge = circulant(th, 0, e, b, k, W - REACH + dx)
            for part, (m, s) in enumerate(zip(split2(main), split2(edge))):
                hb[part, b, e, k, :, 0:W] = m
                hb[part, b, e, k, :, W : 2 * W] = s
            main, edge = circulant(tv, 0, e, b, k, W - REACH + dy)
            for part, (m, s) in enumerate(zip(split2(main), split2(edge))):
                vf[part, b, e, k, :, 0:W] = m
                vf[part, b, e, k, :, W : 2 * W] = s
            main, edge = circulant(tv, 1, e, b, k, W - REACH - dy)
            for part, (m, s) in enumerate(zip(split2(main), split2(edge))):
                vb[part, b, e, k, :, 0:W] = m
                vb[part, b, e, k, :, W : 2 * W] = s
        return carry

    lax.fori_loop(lo, hi, step, 0)


def blocks(top, bottom):
    zero = jnp.zeros((HALF // 2, W), BF16)
    left = jnp.concatenate([top, bottom[0 : HALF // 2], zero], axis=0)
    right = jnp.concatenate([bottom, zero, top[HALF // 2 : HALF]], axis=0)
    return jnp.concatenate([left, right], axis=1)


def side(value):
    return jnp.concatenate([value[0:HALF], value[HALF:ROWS]], axis=1)


def compute_band(b, field, grad, coverage, cv, ov, gv, hf, hb, vf, vb, am, pm):
    main = field[b, 0].reshape(ROWS, W)
    edge = field[b, 1].reshape(ROWS, W)
    x_hi, x_lo = split2(jnp.concatenate([main, edge], axis=1))

    def across(k, carry):
        h_hi, h_lo = hf[0, b, k], hf[1, b, k]
        a = mm(x_hi, h_hi) + mm(x_lo, h_hi) + mm(x_hi, h_lo)
        a_hi, a_lo = split2(a)
        am[0, k] = a_hi
        am[1, k] = a_lo
        return carry

    lax.fori_loop(0, NBASIS, across, 0)

    for e in range(LOCAL):
        cols = slice(e * W, (e + 1) * W)
        model = jnp.zeros((HALF, 2 * W), F32)
        for k in range(NBASIS):
            r_hi = blocks(am[0, k, 0:HALF, cols], am[0, k, HALF:ROWS, cols])
            r_lo = blocks(am[1, k, 0:HALF, cols], am[1, k, HALF:ROWS, cols])
            v_hi, v_lo = vf[0, b, e, k], vf[1, b, e, k]
            down = mm(v_hi, r_hi) + mm(v_hi, r_lo) + mm(v_lo, r_hi)
            model = model + side(cv[e, k]).astype(F32) * down
        weight = (side(gv[e]) * coverage[e, 0]).astype(F32)
        residual = weight * (model - side(ov[e, b]).astype(F32))
        for k in range(NBASIS):
            q_hi, q_lo = split2(side(cv[e, k]).astype(F32) * residual)
            r_hi = blocks(q_hi[:, 0:W], q_hi[:, W : 2 * W])
            r_lo = blocks(q_lo[:, 0:W], q_lo[:, W : 2 * W])
            v_hi, v_lo = vb[0, b, e, k], vb[1, b, e, k]
            up = mm(v_hi, r_hi) + mm(v_hi, r_lo) + mm(v_lo, r_hi)
            for part, p in enumerate(split2(up)):
                at = (e * NBASIS + k) * W
                pm[part, 0:HALF, at : at + W] = p[:, 0:W]
                pm[part, HALF:ROWS, at : at + W] = p[:, W : 2 * W]

    depth = LOCAL * NBASIS * W
    h_hi = hb[0, b].reshape(depth, 2 * W)
    h_lo = hb[1, b].reshape(depth, 2 * W)
    g = mm(pm[0], h_hi) + mm(pm[1], h_hi) + mm(pm[0], h_lo)
    shape = grad.shape[2:]
    grad[b, 0] = g[:, 0:W].reshape(shape)
    grad[b, 1] = g[:, W : 2 * W].reshape(shape)


def kernel(
    scene, kh, kv, coeffs, observed, good, coverage, offsets, out,
    field, left, right, grad, from_core, half, from_x, quarter, from_z, from_left, from_right,
    cv, ov, gv, th, tv, hf, hb, vf, vb, am, pm,
    local_sem, zs, zr, ts, tr, xs, xr, cs, cr, zs2, zr2, ts2, tr2, xs2, xr2, cs2, cr2,
):
    t, me = lax.axis_index("tile"), lax.axis_index("epoch")
    x, z, c = me // (NZ * NC), (me // NC) % NZ, me % NC

    def at(tile, xx, zz, cc):
        return {"tile": tile, "epoch": (xx * NZ + zz) * NC + cc}

    def remote(src, dst, ssem, rsem, where):
        return pltpu.make_async_remote_copy(
            src_ref=src, dst_ref=dst, send_sem=ssem, recv_sem=rsem, device_id=where, device_id_type=MESH
        )

    z_peers = [at(t, x, (z + d) % NZ, c) for d in range(1, NZ)]
    x_peers = [at(t, (x + d) % NX, z, c) for d in range(1, NX)]
    core_peer = at(t, x, z, 1 - c)
    ahead = [at((t + 1) % TILES, x, (z + d) % NZ, c) for d in range(NZ)]
    behind = [at((t + TILES - 1) % TILES, x, (z + d) % NZ, c) for d in range(NZ)]
    everyone = z_peers + x_peers + [core_peer] + ahead + behind

    barrier = pltpu.get_barrier_semaphore()
    for peer in everyone:
        pl.semaphore_signal(barrier, inc=1, device_id=peer, device_id_type=MESH)
    own = pltpu.make_async_copy(scene, field.at[:, 0, x, z, c], local_sem.at[0])
    loads = [
        pltpu.make_async_copy(coeffs, cv, local_sem.at[1]),
        pltpu.make_async_copy(observed, ov, local_sem.at[2]),
        pltpu.make_async_copy(good, gv, local_sem.at[3]),
    ]
    own.start()
    for load in loads:
        load.start()
    own.wait()
    pl.semaphore_wait(barrier, len(everyone))

    mine = field.at[:, 0, x, z, c]
    stage = [remote(mine, mine, zs.at[d], zr.at[d], z_peers[d]) for d in range(NZ - 1)]
    stage += [remote(mine, left.at[:, z], ts.at[d], tr.at[d], ahead[d]) for d in range(NZ)]
    stage += [remote(mine, right.at[:, z], ts.at[NZ + d], tr.at[NZ + d], behind[d]) for d in range(NZ)]
    for copy in stage:
        copy.start()
    prepare_taps(kh, th)
    prepare_taps(kv, tv)
    build_bands(0, 3, offsets, th, tv, hf, hb, vf, vb)
    for copy in stage:
        copy.wait()
    lane = lax.broadcasted_iota(jnp.int32, (BANDS, NZ, 8, W), 3)
    low = jnp.where(t < TILES - 1, right[...], 0.0)
    high = jnp.where(t > 0, left[...], 0.0)
    field[:, 1, x, :, c] = jnp.where(lane < W // 2, low, high)

    mine = field.at[:, :, x, :, c]
    stage = [remote(mine, mine, xs.at[d], xr.at[d], x_peers[d]) for d in range(NX - 1)]
    for copy in stage:
        copy.start()
    build_bands(3, 7, offsets, th, tv, hf, hb, vf, vb)
    for copy in stage:
        copy.wait()

    mine = field.at[:, :, :, :, c]
    copy = remote(mine, mine, cs, cr, core_peer)
    copy.start()
    build_bands(7, BANDS * NBASIS, offsets, th, tv, hf, hb, vf, vb)
    for load in loads:
        load.wait()
    copy.wait()

    def band_step(b, carry):
        compute_band(b, field, grad, coverage, cv, ov, gv, hf, hb, vf, vb, am, pm)
        return carry

    lax.fori_loop(0, BANDS, band_step, 0)

    copy = remote(grad.at[:, :, :, :, 1 - c], from_core, cs2, cr2, core_peer)
    copy.start()
    copy.wait()
    half[...] = grad[:, :, :, :, c] + from_core[...]

    stage = [
        remote(half.at[:, :, (x + d) % NX], from_x.at[d - 1], xs2.at[d - 1], xr2.at[d - 1], x_peers[d - 1])
        for d in range(1, NX)
    ]
    for copy in stage:
        copy.start()
    for copy in stage:
        copy.wait()
    quarter[...] = half[:, :, x] + from_x[0] + from_x[1] + from_x[2]

    stage = [
        remote(quarter.at[:, 0, (z + d) % NZ], from_z.at[d - 1], zs2.at[d - 1], zr2.at[d - 1], z_peers[d - 1])
        for d in range(1, NZ)
    ]
    stage += [
        remote(quarter.at[:, 1, (z + d) % NZ], from_left.at[z], ts2.at[d], tr2.at[d], ahead[d]) for d in range(NZ)
    ]
    stage += [
        remote(quarter.at[:, 1, (z + d) % NZ], from_right.at[z], ts2.at[NZ + d], tr2.at[NZ + d], behind[d])
        for d in range(NZ)
    ]
    for copy in stage:
        copy.start()
    for copy in stage:
        copy.wait()
    lane = lax.broadcasted_iota(jnp.int32, (BANDS, 8, W), 2)
    lower = jnp.where((lane < W // 2) & (t > 0), jnp.sum(from_left[...], axis=0), 0.0)
    upper = jnp.where((lane >= W // 2) & (t < TILES - 1), jnp.sum(from_right[...], axis=0), 0.0)
    out[...] = quarter[:, 0, z] + jnp.sum(from_z[...], axis=0) + lower + upper


def per_device(scene, kernels_h, kernels_v, coeffs, observed, good_pixels, coverage, offsets):
    vmem = pl.BlockSpec(memory_space=pltpu.VMEM)
    smem = pl.BlockSpec(memory_space=pltpu.SMEM)
    hbm = pl.BlockSpec(memory_space=pl.ANY)
    tile = (8, W)
    dma = pltpu.SemaphoreType.DMA
    scratch = [
        pltpu.VMEM((BANDS, 2, NX, NZ, NC) + tile, F32),
        pltpu.VMEM((BANDS, NZ) + tile, F32),
        pltpu.VMEM((BANDS, NZ) + tile, F32),
        pltpu.VMEM((BANDS, 2, NX, NZ, NC) + tile, F32),
        pltpu.VMEM((BANDS, 2, NX, NZ) + tile, F32),
        pltpu.VMEM((BANDS, 2, NX, NZ) + tile, F32),
        pltpu.VMEM((NX - 1, BANDS, 2, NZ) + tile, F32),
        pltpu.VMEM((BANDS, 2, NZ) + tile, F32),
        pltpu.VMEM((NZ - 1, BANDS) + tile, F32),
        pltpu.VMEM((NZ, BANDS) + tile, F32),
        pltpu.VMEM((NZ, BANDS) + tile, F32),
        pltpu.VMEM(coeffs.shape, BF16),
        pltpu.VMEM(observed.shape, BF16),
        pltpu.VMEM(good_pixels.shape, jnp.int32),
        pltpu.VMEM((2, LOCAL, BANDS, 8, W), F32),
        pltpu.VMEM((2, LOCAL, BANDS, 8, W), F32),
        pltpu.VMEM((2, BANDS, NBASIS, 2 * W, LOCAL * W), BF16),
        pltpu.VMEM((2, BANDS, LOCAL, NBASIS, W, 2 * W), BF16),
        pltpu.VMEM((2, BANDS, LOCAL, NBASIS, HALF, 2 * HALF), BF16),
        pltpu.VMEM((2, BANDS, LOCAL, NBASIS, HALF, 2 * HALF), BF16),
        pltpu.VMEM((2, NBASIS, ROWS, LOCAL * W), BF16),
        pltpu.VMEM((2, ROWS, LOCAL * NBASIS * W), BF16),
        dma((4,)),
        dma((NZ - 1,)), dma((NZ - 1,)), dma((2 * NZ,)), dma((2 * NZ,)), dma((NX - 1,)), dma((NX - 1,)), dma, dma,
        dma((NZ - 1,)), dma((NZ - 1,)), dma((2 * NZ,)), dma((2 * NZ,)), dma((NX - 1,)), dma((NX - 1,)), dma, dma,
    ]
    return pl.pallas_call(
        kernel,
        out_shape=jax.ShapeDtypeStruct(scene.shape, F32),
        in_specs=[hbm, vmem, vmem, hbm, hbm, hbm, smem, smem],
        out_specs=vmem,
        scratch_shapes=scratch,
        compiler_params=pltpu.CompilerParams(
            collective_id=0, has_side_effects=True, vmem_limit_bytes=40 * 2**20
        ),
    )(scene, kernels_h, kernels_v, coeffs, observed, good_pixels, coverage, offsets)


def solution(mesh):
    in_specs = (
        P(None, "epoch", "tile"),
        P("epoch", None, None, None),
        P("epoch", None, None, None),
        P("epoch", None, None, "tile"),
        P("epoch", None, None, "tile"),
        P("epoch", None, "tile"),
        P("epoch", "tile"),
        P("epoch", "tile", None),
    )
    out_specs = P(None, "epoch", "tile")
    return jax.shard_map(
        per_device, mesh=mesh, in_specs=in_specs, out_specs=out_specs, check_vma=False
    )
```

```python
import jax
import jax.numpy as jnp
from jax import lax
from jax.experimental import pallas as pl
from jax.experimental.pallas import tpu as pltpu
from jax.sharding import PartitionSpec as P

BANDS, NBASIS, TAPS = 2, 5, 21
LOCAL = 2
ROWS, W, TILES = 256, 128, 8
HALF = 128
REACH = 10
NX, NZ, NC = 4, 4, 2
F32, BF16 = jnp.float32, jnp.bfloat16
MESH = pl.DeviceIdType.MESH


def split2(value):
    hi = value.astype(BF16)
    return hi, (value - hi.astype(F32)).astype(BF16)


def mm(a, b):
    return jnp.dot(a, b, preferred_element_type=F32)


def prepare_taps(taps_in, taps):
    taps[...] = jnp.zeros_like(taps)
    lane = lax.broadcasted_iota(jnp.int32, (8, W), 1)
    for e in range(LOCAL):
        for b in range(BANDS):
            taps[0, e, b, 0:NBASIS, 0:TAPS] = taps_in[e, :, b, :]

    def step(i, carry):
        row = taps[0, i // BANDS, i % BANDS]
        back = jnp.zeros((8, W), F32)
        for a in range(TAPS):
            back = jnp.where(lane == TAPS - 1 - a, row[:, a : a + 1], back)
        taps[1, i // BANDS, i % BANDS] = back
        return carry

    lax.fori_loop(0, LOCAL * BANDS, step, 0)


def build_bands(offsets, th, tv, hf, hb, vf, vb):
    row = lax.broadcasted_iota(jnp.int32, (W, W), 0)
    lane = lax.broadcasted_iota(jnp.int32, (W, W), 1)
    near = jnp.abs(row - lane) < W // 2

    def circulant(taps, flipped, e, b, k, shift):
        base = jnp.broadcast_to(taps[flipped, e, b, pl.ds(k, 1), :], (8, W))
        for bit in (1, 2, 4):
            base = jnp.where((row[0:8] & bit) != 0, pltpu.roll(base, bit, axis=1), base)
        base = pltpu.roll(base, shift, axis=1)
        full = jnp.concatenate([base] + [pltpu.roll(base, g, axis=1) for g in range(8, W, 8)], axis=0)
        return split2(jnp.where(near, full, 0.0)), split2(jnp.where(near, 0.0, full))

    def step(i, carry):
        b, k = i // NBASIS, i % NBASIS
        first = pl.ds(pl.multiple_of(b * (W // 2), W // 2), W // 2)
        second = pl.ds(pl.multiple_of((1 - b) * (W // 2), W // 2), W // 2)
        for e in range(LOCAL):
            dy, dx = offsets[e, 0, 0], offsets[e, 0, 1]
            cols = slice(e * W, (e + 1) * W)
            main, edge = circulant(th, 1, e, b, k, W - REACH - dx)
            for part in range(2):
                hf[part, b, k, 0, :, cols] = main[part]
                hf[part, b, k, 1, first, cols] = edge[part][0 : W // 2]
                hf[part, b, k, 1, second, cols] = edge[part][W // 2 : W]
            main, edge = circulant(th, 0, e, b, k, W - REACH + dx)
            for part in range(2):
                hb[part, b, e, k, :, 0:W] = main[part]
                hb[part, b, e, k, :, W : 2 * W] = edge[part]
            main, edge = circulant(tv, 0, e, b, k, W - REACH + dy)
            for part in range(2):
                vf[part, b, e, k, :, 0:W] = main[part]
                vf[part, b, e, k, :, W : 2 * W] = edge[part]
            main, edge = circulant(tv, 1, e, b, k, W - REACH - dy)
            for part in range(2):
                vb[part, b, e, k, :, 0:W] = main[part]
                vb[part, b, e, k, :, W : 2 * W] = edge[part]
        return carry

    lax.fori_loop(0, BANDS * NBASIS, step, 0)


def blocks(top, bottom):
    zero = jnp.zeros((HALF // 2, W), BF16)
    left = jnp.concatenate([top, bottom[0 : HALF // 2], zero], axis=0)
    right = jnp.concatenate([bottom, zero, top[HALF // 2 : HALF]], axis=0)
    return jnp.concatenate([left, right], axis=1)


def side(value):
    return jnp.concatenate([value[0:HALF], value[HALF:ROWS]], axis=1)


def mm3(a, b):
    if a[0].shape[1] < 2 * W:
        wide = mm(jnp.concatenate(a, axis=1), jnp.concatenate([b[0], b[0]], axis=0))
        return wide + mm(a[0], b[1])
    return mm(a[0], b[0]) + mm(a[1], b[0]) + mm(a[0], b[1])


def both(ref, *index):
    return ref[(0,) + index], ref[(1,) + index]


def epoch_terms(b, e, coverage, cv, ov, gv, vf, vb, am, pm):
    model = jnp.zeros((HALF, 2 * W), F32)
    for k in range(NBASIS):
        rows = [blocks(am[part, b, e, k, 0:HALF], am[part, b, e, k, HALF:ROWS]) for part in range(2)]
        model = model + side(cv[e, k]).astype(F32) * mm3(both(vf, b, e, k), rows)
    weight = (side(gv[e]) * coverage[0, e]).astype(F32)
    residual = weight * (model - side(ov[e, b]).astype(F32))
    for k in range(NBASIS):
        q = split2(side(cv[e, k]).astype(F32) * residual)
        rows = [blocks(part[:, 0:W], part[:, W : 2 * W]) for part in q]
        up = mm3(both(vb, b, e, k), rows)
        for part, p in enumerate(split2(up)):
            pm[part, e * NBASIS + k, 0:HALF] = p[:, 0:W]
            pm[part, e * NBASIS + k, HALF:ROWS] = p[:, W : 2 * W]


def kernel(
    scene, kh, kv, coeffs, observed, good, coverage_in, offsets_in, out,
    field, packed, sides, left, right, grad, from_core, half, from_e, from_left, from_right,
    khv, kvv, cv, ov, gv, coverage, offsets, th, tv, hf, hb, vf, vb, af, am, pm,
    local_sem, es, er, ss, sr, cs, cr, es2, er2, ss2, sr2, cs2, cr2,
):
    t, me = lax.axis_index("tile"), lax.axis_index("epoch")
    x, z, c = me // (NZ * NC), (me // NC) % NZ, me % NC

    def at(tile, xx, zz, cc):
        return {"tile": tile, "epoch": (xx * NZ + zz) * NC + cc}

    def remote(src, dst, ssem, rsem, where):
        return pltpu.make_async_remote_copy(
            src_ref=src, dst_ref=dst, send_sem=ssem, recv_sem=rsem, device_id=where, device_id_type=MESH
        )

    def signal(where):
        pl.semaphore_signal(barrier, inc=1, device_id=where, device_id_type=MESH)

    spots = [((x + i) % NX, (z + j) % NZ) for i in range(NX) for j in range(NZ)]
    spots = spots[1:] + spots[:1]
    near = NX * NZ - 1
    has_left, has_right = t > 0, t < TILES - 1

    barrier = pltpu.get_barrier_semaphore()
    own = pltpu.make_async_copy(scene, field.at[:, x, z, c], local_sem.at[0])
    own.start()
    @pl.when(has_right)
    def _():
        for xx, zz in spots:
            signal(at(t + 1, xx, zz, c))

    @pl.when(has_left)
    def _():
        for xx, zz in spots:
            signal(at(t - 1, xx, zz, c))

    for xx, zz in spots[:near]:
        signal(at(t, xx, zz, c))
    signal(at(t, x, z, 1 - c))

    small = [
        pltpu.make_async_copy(kh, khv, local_sem.at[1]),
        pltpu.make_async_copy(kv, kvv, local_sem.at[2]),
        pltpu.make_async_copy(coverage_in, coverage, local_sem.at[3]),
        pltpu.make_async_copy(offsets_in, offsets, local_sem.at[4]),
    ]
    loads = [
        pltpu.make_async_copy(coeffs, cv, local_sem.at[5]),
        pltpu.make_async_copy(observed, ov, local_sem.at[6]),
        pltpu.make_async_copy(good, gv, local_sem.at[7]),
    ]
    for load in small + loads:
        load.start()
    own.wait()
    lane = lax.broadcasted_iota(jnp.int32, (8, W), 1)
    outer = (lane < W // 4) | (lane >= 3 * W // 4)
    turned = pltpu.roll(field[1, x, z, c], W // 2, axis=1)
    packed[...] = jnp.where(outer, field[0, x, z, c], turned)
    count = near + 1 + len(spots) * (has_left.astype(jnp.int32) + has_right.astype(jnp.int32))
    pl.semaphore_wait(barrier, count)

    mine = field.at[:, x, z, c]
    mains = [remote(mine, mine, es.at[d], er.at[d], at(t, *spots[d], c)) for d in range(near)]
    n = len(spots)
    slot = x * NZ + z
    to_right = [remote(packed, left.at[slot], ss.at[d], sr.at[d], at(t + 1, *spots[d], c)) for d in range(n)]
    to_left = [remote(packed, right.at[slot], ss.at[n + d], sr.at[n + d], at(t - 1, *spots[d], c)) for d in range(n)]
    @pl.when(has_right)
    def _():
        for copy in to_right:
            copy.start()

    @pl.when(has_left)
    def _():
        for copy in to_left:
            copy.start()

    for copy in mains:
        copy.start()

    for load in small:
        load.wait()
    prepare_taps(khv, th)
    prepare_taps(kvv, tv)
    build_bands(offsets, th, tv, hf, hb, vf, vb)
    for copy in mains:
        copy.wait_recv()
    rows = field.at[:, :, :, c]
    swap = remote(rows, rows, cs.at[0], cr.at[0], at(t, x, z, 1 - c))
    swap.start()
    for load in loads:
        load.wait()

    @pl.when(has_left)
    def _():
        for copy in to_right:
            copy.wait_recv()

    @pl.when(has_right)
    def _():
        for copy in to_left:
            copy.wait_recv()

    lane = lax.broadcasted_iota(jnp.int32, (n, 8, W), 2)
    from_right_side = (lane // (W // 4)) % 2 == 0
    low = jnp.where(has_right, right[...], 0.0)
    high = jnp.where(has_left, left[...], 0.0)
    sides[:, :, c] = jnp.where(from_right_side, low, high).reshape(NX, NZ, 8, W)
    rows = sides.at[:, :, c]
    swap_sides = remote(rows, rows, cs.at[1], cr.at[1], at(t, x, z, 1 - c))
    swap_sides.start()

    swap.wait_recv()
    parts = [split2(field[b].reshape(ROWS, W)) for b in range(BANDS)]

    def own_columns(k, carry):
        for b in range(BANDS):
            af[b, k] = mm3(parts[b], both(hf, b, k, 0))
        return carry

    lax.fori_loop(0, NBASIS, own_columns, 0)
    swap_sides.wait_recv()
    beside = split2(sides[...].reshape(ROWS, W))

    def side_columns(k, carry):
        for b in range(BANDS):
            a = split2(af[b, k] + mm3(beside, both(hf, b, k, 1)))
            for part in range(2):
                for e in range(LOCAL):
                    am[part, b, e, k] = a[part][:, e * W : (e + 1) * W]
        return carry

    lax.fori_loop(0, NBASIS, side_columns, 0)

    depth = LOCAL * NBASIS * W
    shape = grad.shape[1:]

    def across(b, lo):
        h = [hb[part, b, :, :, :, lo : lo + W].reshape(depth, W) for part in range(2)]
        p = [jnp.concatenate([pm[part, i] for i in range(LOCAL * NBASIS)], axis=1) for part in range(2)]
        return mm3(p, h)

    def sum_copy(b):
        return remote(grad.at[b, :, :, 1 - c], from_core.at[b], cs2.at[b], cr2.at[b], at(t, x, z, 1 - c))

    def take_sum(b):
        sum_copy(b).wait_recv()
        half[b] = grad[b, :, :, c] + from_core[b]

    def mains_of(b):
        return [
            remote(half.at[b, spots[d][0], spots[d][1]], from_e.at[b, d], es2.at[b, d], er2.at[b, d], at(t, *spots[d], c))
            for d in range(near)
        ]

    mains0, mains1 = mains_of(0), mains_of(1)
    wide = lax.broadcasted_iota(jnp.int32, (ROWS, W), 1)
    wide = (wide < W // 4) | (wide >= 3 * W // 4)

    def band_step(b, carry):
        def epoch_step(e, carry):
            epoch_terms(b, e, coverage, cv, ov, gv, vf, vb, am, pm)

            @pl.when((b == 1) & (e == 1))
            def _():
                take_sum(0)
                for copy in mains0:
                    copy.start()

            return carry

        lax.fori_loop(0, LOCAL, epoch_step, 0)
        edge = across(b, W)

        @pl.when(b == 0)
        def _():
            grad[BANDS] = edge.reshape(shape)

        @pl.when(b == 1)
        def _():
            first = grad[BANDS].reshape(ROWS, W)
            grad[BANDS] = jnp.where(wide, first, pltpu.roll(edge, W // 2, axis=1)).reshape(shape)
            sum_copy(BANDS).start()

        grad[b] = across(b, 0).reshape(shape)
        sum_copy(b).start()
        return carry

    lax.fori_loop(0, BANDS, band_step, 0)
    take_sum(BANDS)
    to_right2 = [
        remote(half.at[2, spots[d][0], spots[d][1]], from_left.at[slot], ss2.at[d], sr2.at[d], at(t + 1, *spots[d], c))
        for d in range(n)
    ]
    to_left2 = [
        remote(
            half.at[2, spots[d][0], spots[d][1]], from_right.at[slot], ss2.at[n + d], sr2.at[n + d], at(t - 1, *spots[d], c)
        )
        for d in range(n)
    ]

    @pl.when(has_right)
    def _():
        for copy in to_right2:
            copy.start()

    @pl.when(has_left)
    def _():
        for copy in to_left2:
            copy.start()

    take_sum(1)
    for copy in mains1:
        copy.start()

    for copy in mains + [swap, swap_sides] + [sum_copy(b) for b in range(BANDS + 1)] + mains0 + mains1:
        copy.wait_send()

    @pl.when(has_right)
    def _():
        for copy in to_right + to_right2:
            copy.wait_send()

    @pl.when(has_left)
    def _():
        for copy in to_left + to_left2:
            copy.wait_send()

    for copy in mains0 + mains1:
        copy.wait_recv()

    @pl.when(has_left)
    def _():
        for copy in to_right2:
            copy.wait_recv()

    @pl.when(has_right)
    def _():
        for copy in to_left2:
            copy.wait_recv()

    lane = lax.broadcasted_iota(jnp.int32, (8, W), 1)
    lower = jnp.where(has_left, jnp.sum(from_left[...], axis=0), 0.0)
    upper = jnp.where(has_right, jnp.sum(from_right[...], axis=0), 0.0)
    beside = jnp.where((lane // (W // 4)) % 2 == 0, lower, upper)
    for b in range(BANDS):
        add = beside if b == 0 else pltpu.roll(beside, W // 2, axis=1)
        out[b] = half[b, x, z] + jnp.sum(from_e[b], axis=0) + jnp.where(outer, add, 0.0)


def per_device(scene, kernels_h, kernels_v, coeffs, observed, good_pixels, coverage, offsets):
    vmem = pl.BlockSpec(memory_space=pltpu.VMEM)
    hbm = pl.BlockSpec(memory_space=pl.ANY)
    tile = (8, W)
    dma = pltpu.SemaphoreType.DMA
    chips = (NX, NZ)
    n = NX * NZ
    scratch = [
        pltpu.VMEM((BANDS, *chips, NC) + tile, F32),
        pltpu.VMEM(tile, F32),
        pltpu.VMEM((*chips, NC) + tile, F32),
        pltpu.VMEM((n,) + tile, F32),
        pltpu.VMEM((n,) + tile, F32),
        pltpu.VMEM((BANDS + 1, *chips, NC) + tile, F32),
        pltpu.VMEM((BANDS + 1, *chips) + tile, F32),
        pltpu.VMEM((BANDS + 1, *chips) + tile, F32),
        pltpu.VMEM((BANDS, n - 1) + tile, F32),
        pltpu.VMEM((n,) + tile, F32),
        pltpu.VMEM((n,) + tile, F32),
        pltpu.VMEM((LOCAL, NBASIS, BANDS, TAPS), F32),
        pltpu.VMEM((LOCAL, NBASIS, BANDS, TAPS), F32),
        pltpu.VMEM(coeffs.shape, BF16),
        pltpu.VMEM(observed.shape, BF16),
        pltpu.VMEM(good_pixels.shape, jnp.int32),
        pltpu.SMEM((1, LOCAL), jnp.int32),
        pltpu.SMEM(offsets.shape, jnp.int32),
        pltpu.VMEM((2, LOCAL, BANDS, 8, W), F32),
        pltpu.VMEM((2, LOCAL, BANDS, 8, W), F32),
        pltpu.VMEM((2, BANDS, NBASIS, 2, W, LOCAL * W), BF16),
        pltpu.VMEM((2, BANDS, LOCAL, NBASIS, W, 2 * W), BF16),
        pltpu.VMEM((2, BANDS, LOCAL, NBASIS, HALF, 2 * HALF), BF16),
        pltpu.VMEM((2, BANDS, LOCAL, NBASIS, HALF, 2 * HALF), BF16),
        pltpu.VMEM((BANDS, NBASIS, ROWS, LOCAL * W), F32),
        pltpu.VMEM((2, BANDS, LOCAL, NBASIS, ROWS, W), BF16),
        pltpu.VMEM((2, LOCAL * NBASIS, ROWS, W), BF16),
        dma((8,)),
        dma((n - 1,)), dma((n - 1,)), dma((2 * n,)), dma((2 * n,)), dma((2,)), dma((2,)),
        dma((BANDS, n - 1)), dma((BANDS, n - 1)), dma((2 * n,)), dma((2 * n,)), dma((BANDS + 1,)), dma((BANDS + 1,)),
    ]
    return pl.pallas_call(
        kernel,
        out_shape=jax.ShapeDtypeStruct(scene.shape, F32),
        in_specs=[hbm] * 8,
        out_specs=vmem,
        scratch_shapes=scratch,
        compiler_params=pltpu.CompilerParams(
            collective_id=0, has_side_effects=True, vmem_limit_bytes=60 * 2**20
        ),
    )(
        scene,
        kernels_h.transpose(0, 2, 1, 3),
        kernels_v.transpose(0, 2, 1, 3),
        coeffs,
        observed,
        good_pixels,
        coverage.transpose(1, 0),
        offsets,
    )


def solution(mesh):
    in_specs = (
        P(None, "epoch", "tile"),
        P("epoch", None, None, None),
        P("epoch", None, None, None),
        P("epoch", None, None, "tile"),
        P("epoch", None, None, "tile"),
        P("epoch", None, "tile"),
        P("epoch", "tile"),
        P("epoch", "tile", None),
    )
    out_specs = P(None, "epoch", "tile")
    return jax.shard_map(
        per_device, mesh=mesh, in_specs=in_specs, out_specs=out_specs, check_vma=False
    )
```

```python
import jax
import jax.numpy as jnp
from jax import lax
from jax.experimental import pallas as pl
from jax.experimental.pallas import tpu as pltpu
from jax.sharding import PartitionSpec as P

BANDS, NBASIS, TAPS = 2, 5, 21
LOCAL = 2
ROWS, W, TILES = 256, 128, 8
HALF = 128
REACH = 10
NX, NZ, NC = 4, 4, 2
F32, BF16 = jnp.float32, jnp.bfloat16
MESH = pl.DeviceIdType.MESH


def split2(value):
    hi = value.astype(BF16)
    return hi, (value - hi.astype(F32)).astype(BF16)


def mm(a, b):
    return jnp.dot(a, b, preferred_element_type=F32)


def prepare_taps(taps_in, taps):
    taps[...] = jnp.zeros_like(taps)
    lane = lax.broadcasted_iota(jnp.int32, (8, W), 1)
    for e in range(LOCAL):
        for b in range(BANDS):
            taps[0, e, b, 0:NBASIS, 0:TAPS] = taps_in[e, :, b, :]

    def step(i, carry):
        row = taps[0, i // BANDS, i % BANDS]
        back = jnp.zeros((8, W), F32)
        for a in range(TAPS):
            back = jnp.where(lane == TAPS - 1 - a, row[:, a : a + 1], back)
        taps[1, i // BANDS, i % BANDS] = back
        return carry

    lax.fori_loop(0, LOCAL * BANDS, step, 0)


def build_bands(offsets, th, tv, hf, hb, vf, vb):
    row = lax.broadcasted_iota(jnp.int32, (W, W), 0)
    lane = lax.broadcasted_iota(jnp.int32, (W, W), 1)
    near = jnp.abs(row - lane) < W // 2

    def circulant(taps, flipped, e, b, k, shift):
        base = jnp.broadcast_to(taps[flipped, e, b, pl.ds(k, 1), :], (8, W))
        for bit in (1, 2, 4):
            base = jnp.where((row[0:8] & bit) != 0, pltpu.roll(base, bit, axis=1), base)
        base = pltpu.roll(base, shift, axis=1)
        full = jnp.concatenate([base] + [pltpu.roll(base, g, axis=1) for g in range(8, W, 8)], axis=0)
        return split2(jnp.where(near, full, 0.0)), split2(jnp.where(near, 0.0, full))

    def step(i, carry):
        b, k = i // NBASIS, i % NBASIS
        first = pl.ds(pl.multiple_of(b * (W // 2), W // 2), W // 2)
        second = pl.ds(pl.multiple_of((1 - b) * (W // 2), W // 2), W // 2)
        for e in range(LOCAL):
            dy, dx = offsets[e, 0, 0], offsets[e, 0, 1]
            cols = slice(e * W, (e + 1) * W)
            main, edge = circulant(th, 1, e, b, k, W - REACH - dx)
            for part in range(2):
                hf[part, b, k, 0, :, cols] = main[part]
                hf[part, b, k, 1, first, cols] = edge[part][0 : W // 2]
                hf[part, b, k, 1, second, cols] = edge[part][W // 2 : W]
            main, edge = circulant(th, 0, e, b, k, W - REACH + dx)
            for part in range(2):
                hb[part, b, e, k, :, 0:W] = main[part]
                hb[part, b, e, k, :, W : 2 * W] = edge[part]
            main, edge = circulant(tv, 0, e, b, k, W - REACH + dy)
            for part in range(2):
                vf[part, b, e, k, :, 0:W] = main[part]
                vf[part, b, e, k, :, W : 2 * W] = edge[part]
            main, edge = circulant(tv, 1, e, b, k, W - REACH - dy)
            for part in range(2):
                vb[part, b, e, k, :, 0:W] = main[part]
                vb[part, b, e, k, :, W : 2 * W] = edge[part]
        return carry

    lax.fori_loop(0, BANDS * NBASIS, step, 0)


def blocks(top, bottom):
    zero = jnp.zeros((HALF // 2, W), BF16)
    left = jnp.concatenate([top, bottom[0 : HALF // 2], zero], axis=0)
    right = jnp.concatenate([bottom, zero, top[HALF // 2 : HALF]], axis=0)
    return jnp.concatenate([left, right], axis=1)


def side(value):
    return jnp.concatenate([value[0:HALF], value[HALF:ROWS]], axis=1)


def mm3(a, b):
    if a[0].shape[1] < 2 * W:
        wide = mm(jnp.concatenate(a, axis=1), jnp.concatenate([b[0], b[0]], axis=0))
        return wide + mm(a[0], b[1])
    if a[0].shape[1] > 2 * W:
        return mm(a[0], b[0]) + mm(a[1], b[0]) + mm(a[0], b[1])
    rows = a[0].shape[0]
    tall = mm(jnp.concatenate(a, axis=0), b[0])
    return tall[0:rows] + tall[rows:] + mm(a[0], b[1])


def both(ref, *index):
    return ref[(0,) + index], ref[(1,) + index]


def epoch_terms(b, e, coverage, cv, ov, gv, vf, vb, am, pm):
    model = jnp.zeros((HALF, 2 * W), F32)
    for k in range(NBASIS):
        rows = [blocks(am[part, b, e, k, 0:HALF], am[part, b, e, k, HALF:ROWS]) for part in range(2)]
        model = model + side(cv[e, k]).astype(F32) * mm3(both(vf, b, e, k), rows)
    weight = (side(gv[e]) * coverage[0, e]).astype(F32)
    residual = weight * (model - side(ov[e, b]).astype(F32))
    for k in range(NBASIS):
        q = split2(side(cv[e, k]).astype(F32) * residual)
        rows = [blocks(part[:, 0:W], part[:, W : 2 * W]) for part in q]
        up = mm3(both(vb, b, e, k), rows)
        for part, p in enumerate(split2(up)):
            pm[part, e * NBASIS + k, 0:HALF] = p[:, 0:W]
            pm[part, e * NBASIS + k, HALF:ROWS] = p[:, W : 2 * W]


def right_lanes(shape):
    return (lax.broadcasted_iota(jnp.int32, shape, len(shape) - 1) // (W // 4)) % 2 == 0


def fold(value, to_right):
    axis = value.ndim - 1
    below = pltpu.roll(value, 4, axis=axis - 1)
    below = pltpu.roll(below, W // 4 if to_right else 3 * W // 4, axis=axis)
    mixed = jnp.where(right_lanes(value.shape) == to_right, value, below)
    return mixed[..., 0:4, :]


def unfold(value, to_right):
    return pltpu.roll(value, 3 * W // 4 if to_right else W // 4, axis=value.ndim - 1)


def kernel(
    scene, kh, kv, coeffs, observed, good, coverage_in, offsets_in, out,
    field, packed_right, packed_left, sides, left, right, grad, from_core, half, from_e, half_right, half_left, from_left, from_right,
    khv, kvv, cv, ov, gv, coverage, offsets, th, tv, hf, hb, vf, vb, af, am, pm, beside,
    local_sem, es, er, ss, sr, cs, cr, es2, er2, ss2, sr2, cs2, cr2,
):
    t, me = lax.axis_index("tile"), lax.axis_index("epoch")
    x, z, c = me // (NZ * NC), (me // NC) % NZ, me % NC

    def at(tile, xx, zz, cc):
        return {"tile": tile, "epoch": (xx * NZ + zz) * NC + cc}

    def remote(src, dst, ssem, rsem, where):
        return pltpu.make_async_remote_copy(
            src_ref=src, dst_ref=dst, send_sem=ssem, recv_sem=rsem, device_id=where, device_id_type=MESH
        )

    def signal(where):
        pl.semaphore_signal(barrier, inc=1, device_id=where, device_id_type=MESH)

    spots = [((x + i) % NX, (z + j) % NZ) for i in (2, 1, 3, 0) for j in (2, 1, 3, 0)]
    near = NX * NZ - 1
    has_left, has_right = t > 0, t < TILES - 1

    barrier = pltpu.get_barrier_semaphore()
    own = pltpu.make_async_copy(scene, field.at[:, x, z, c], local_sem.at[0])
    own.start()
    @pl.when(has_right)
    def _():
        for xx, zz in spots:
            signal(at(t + 1, xx, zz, c))

    @pl.when(has_left)
    def _():
        for xx, zz in spots:
            signal(at(t - 1, xx, zz, c))

    for xx, zz in spots[:near]:
        signal(at(t, xx, zz, c))
    signal(at(t, x, z, 1 - c))

    small = [
        pltpu.make_async_copy(kh, khv, local_sem.at[1]),
        pltpu.make_async_copy(kv, kvv, local_sem.at[2]),
        pltpu.make_async_copy(coverage_in, coverage, local_sem.at[3]),
        pltpu.make_async_copy(offsets_in, offsets, local_sem.at[4]),
    ]
    loads = [
        pltpu.make_async_copy(coeffs, cv, local_sem.at[5]),
        pltpu.make_async_copy(observed, ov, local_sem.at[6]),
        pltpu.make_async_copy(good, gv, local_sem.at[7]),
    ]
    for load in small + loads:
        load.start()
    own.wait()
    lane = lax.broadcasted_iota(jnp.int32, (8, W), 1)
    outer = (lane < W // 4) | (lane >= 3 * W // 4)
    turned = pltpu.roll(field[1, x, z, c], W // 2, axis=1)
    packed = jnp.where(outer, field[0, x, z, c], turned)
    packed_right[...] = fold(packed, True)
    packed_left[...] = fold(packed, False)
    for load in small:
        load.wait()
    prepare_taps(khv, th)
    prepare_taps(kvv, tv)
    count = near + 1 + len(spots) * (has_left.astype(jnp.int32) + has_right.astype(jnp.int32))
    pl.semaphore_wait(barrier, count)

    mine = field.at[:, x, z, c]
    mains = [remote(mine, mine, es.at[d], er.at[d], at(t, *spots[d], c)) for d in range(near)]
    n = len(spots)
    slot = x * NZ + z
    to_right = [remote(packed_left, left.at[slot], ss.at[d], sr.at[d], at(t + 1, *spots[d], c)) for d in range(n)]
    to_left = [remote(packed_right, right.at[slot], ss.at[n + d], sr.at[n + d], at(t - 1, *spots[d], c)) for d in range(n)]
    @pl.when(has_right)
    def _():
        for copy in to_right:
            copy.start()

    @pl.when(has_left)
    def _():
        for copy in to_left:
            copy.start()

    for copy in mains:
        copy.start()

    build_bands(offsets, th, tv, hf, hb, vf, vb)
    for copy in mains:
        copy.wait_recv()
    rows = field.at[:, :, :, c]
    swap = remote(rows, rows, cs.at[0], cr.at[0], at(t, x, z, 1 - c))
    swap.start()
    for load in loads:
        load.wait()

    @pl.when(has_left)
    def _():
        for copy in to_right:
            copy.wait_recv()

    @pl.when(has_right)
    def _():
        for copy in to_left:
            copy.wait_recv()

    low = jnp.where(has_right, right[...], 0.0)
    high = jnp.where(has_left, left[...], 0.0)
    mask = right_lanes((n, 4, W))
    sides[:, :, c, 0:4] = jnp.where(mask, low, high).reshape(NX, NZ, 4, W)
    sides[:, :, c, 4:8] = jnp.where(mask, unfold(low, True), unfold(high, False)).reshape(NX, NZ, 4, W)
    rows = sides.at[:, :, c]
    swap_sides = remote(rows, rows, cs.at[1], cr.at[1], at(t, x, z, 1 - c))
    swap_sides.start()

    swap.wait_recv()
    parts = [split2(field[b].reshape(ROWS, W)) for b in range(BANDS)]

    def own_columns(k, carry):
        for b in range(BANDS):
            af[b, k] = mm3(parts[b], both(hf, b, k, 0))
        return carry

    lax.fori_loop(0, NBASIS, own_columns, 0, unroll=True)
    swap_sides.wait_recv()
    side_parts = split2(sides[...].reshape(ROWS, W))

    def side_columns(k, carry):
        for b in range(BANDS):
            a = split2(af[b, k] + mm3(side_parts, both(hf, b, k, 1)))
            for part in range(2):
                for e in range(LOCAL):
                    am[part, b, e, k] = a[part][:, e * W : (e + 1) * W]
        return carry

    lax.fori_loop(0, NBASIS, side_columns, 0, unroll=True)

    depth = LOCAL * NBASIS * W
    shape = grad.shape[1:]

    def across(b):
        h = [hb[part, b].reshape(depth, 2 * W) for part in range(2)]
        p = [jnp.concatenate([pm[part, i] for i in range(LOCAL * NBASIS)], axis=1) for part in range(2)]
        return mm3(p, h)

    def sum_copy(b):
        return remote(grad.at[b, :, :, 1 - c], from_core.at[b], cs2.at[b], cr2.at[b], at(t, x, z, 1 - c))

    def take_sum(b):
        sum_copy(b).wait_recv()
        half[b] = grad[b, :, :, c] + from_core[b]

    def mains_of(b):
        return [
            remote(half.at[b, spots[d][0], spots[d][1]], from_e.at[b, d], es2.at[b, d], er2.at[b, d], at(t, *spots[d], c))
            for d in range(near)
        ]

    mains0, mains1 = mains_of(0), mains_of(1)
    wide = lax.broadcasted_iota(jnp.int32, (ROWS, W), 1)
    wide = (wide < W // 4) | (wide >= 3 * W // 4)

    def band_step(b, carry):
        def epoch_step(e, carry):
            epoch_terms(b, e, coverage, cv, ov, gv, vf, vb, am, pm)

            @pl.when((b == 1) & (e == 1))
            def _():
                take_sum(0)
                for copy in mains0:
                    copy.start()

            return carry

        lax.fori_loop(0, LOCAL, epoch_step, 0)
        full = across(b)
        edge = full[:, W : 2 * W]

        @pl.when(b == 0)
        def _():
            grad[BANDS] = edge.reshape(shape)

        @pl.when(b == 1)
        def _():
            first = grad[BANDS].reshape(ROWS, W)
            grad[BANDS] = jnp.where(wide, first, pltpu.roll(edge, W // 2, axis=1)).reshape(shape)
            sum_copy(BANDS).start()

        grad[b] = full[:, 0:W].reshape(shape)
        sum_copy(b).start()
        return carry

    lax.fori_loop(0, BANDS, band_step, 0)
    take_sum(BANDS)
    strips = half[BANDS].reshape(n, 8, W)
    half_right[...] = fold(strips, True).reshape(NX, NZ, 4, W)
    half_left[...] = fold(strips, False).reshape(NX, NZ, 4, W)
    to_right2 = [
        remote(half_right.at[spots[d][0], spots[d][1]], from_left.at[slot], ss2.at[d], sr2.at[d], at(t + 1, *spots[d], c))
        for d in range(n)
    ]
    to_left2 = [
        remote(
            half_left.at[spots[d][0], spots[d][1]], from_right.at[slot], ss2.at[n + d], sr2.at[n + d], at(t - 1, *spots[d], c)
        )
        for d in range(n)
    ]

    @pl.when(has_right)
    def _():
        for copy in to_right2:
            copy.start()

    @pl.when(has_left)
    def _():
        for copy in to_left2:
            copy.start()

    take_sum(1)
    for copy in mains1:
        copy.start()

    for copy in mains + [swap, swap_sides] + [sum_copy(b) for b in range(BANDS + 1)] + mains0 + mains1:
        copy.wait_send()

    @pl.when(has_right)
    def _():
        for copy in to_right + to_right2:
            copy.wait_send()

    @pl.when(has_left)
    def _():
        for copy in to_left + to_left2:
            copy.wait_send()

    for copy in mains0 + mains1:
        copy.wait_recv()

    @pl.when(has_left)
    def _():
        for copy in to_right2:
            copy.wait_recv()

    @pl.when(has_right)
    def _():
        for copy in to_left2:
            copy.wait_recv()

    lane = lax.broadcasted_iota(jnp.int32, (8, W), 1)
    lower = jnp.where(has_left, jnp.sum(from_left[...], axis=0), 0.0)
    upper = jnp.where(has_right, jnp.sum(from_right[...], axis=0), 0.0)
    mask = right_lanes((4, W))
    beside[0:4] = jnp.where(mask, lower, upper)
    beside[4:8] = jnp.where(mask, unfold(lower, True), unfold(upper, False))
    for b in range(BANDS):
        add = beside[...] if b == 0 else pltpu.roll(beside[...], W // 2, axis=1)
        out[b] = half[b, x, z] + jnp.sum(from_e[b], axis=0) + jnp.where(outer, add, 0.0)


def per_device(scene, kernels_h, kernels_v, coeffs, observed, good_pixels, coverage, offsets):
    vmem = pl.BlockSpec(memory_space=pltpu.VMEM)
    hbm = pl.BlockSpec(memory_space=pl.ANY)
    tile = (8, W)
    dma = pltpu.SemaphoreType.DMA
    chips = (NX, NZ)
    n = NX * NZ
    scratch = [
        pltpu.VMEM((BANDS, *chips, NC) + tile, F32),
        pltpu.VMEM((4, W), F32),
        pltpu.VMEM((4, W), F32),
        pltpu.VMEM((*chips, NC) + tile, F32),
        pltpu.VMEM((n, 4, W), F32),
        pltpu.VMEM((n, 4, W), F32),
        pltpu.VMEM((BANDS + 1, *chips, NC) + tile, F32),
        pltpu.VMEM((BANDS + 1, *chips) + tile, F32),
        pltpu.VMEM((BANDS + 1, *chips) + tile, F32),
        pltpu.VMEM((BANDS, n - 1) + tile, F32),
        pltpu.VMEM((*chips, 4, W), F32),
        pltpu.VMEM((*chips, 4, W), F32),
        pltpu.VMEM((n, 4, W), F32),
        pltpu.VMEM((n, 4, W), F32),
        pltpu.VMEM((LOCAL, NBASIS, BANDS, TAPS), F32),
        pltpu.VMEM((LOCAL, NBASIS, BANDS, TAPS), F32),
        pltpu.VMEM(coeffs.shape, BF16),
        pltpu.VMEM(observed.shape, BF16),
        pltpu.VMEM(good_pixels.shape, jnp.int32),
        pltpu.SMEM((1, LOCAL), jnp.int32),
        pltpu.SMEM(offsets.shape, jnp.int32),
        pltpu.VMEM((2, LOCAL, BANDS, 8, W), F32),
        pltpu.VMEM((2, LOCAL, BANDS, 8, W), F32),
        pltpu.VMEM((2, BANDS, NBASIS, 2, W, LOCAL * W), BF16),
        pltpu.VMEM((2, BANDS, LOCAL, NBASIS, W, 2 * W), BF16),
        pltpu.VMEM((2, BANDS, LOCAL, NBASIS, HALF, 2 * HALF), BF16),
        pltpu.VMEM((2, BANDS, LOCAL, NBASIS, HALF, 2 * HALF), BF16),
        pltpu.VMEM((BANDS, NBASIS, ROWS, LOCAL * W), F32),
        pltpu.VMEM((2, BANDS, LOCAL, NBASIS, ROWS, W), BF16),
        pltpu.VMEM((2, LOCAL * NBASIS, ROWS, W), BF16),
        pltpu.VMEM(tile, F32),
        dma((8,)),
        dma((n - 1,)), dma((n - 1,)), dma((2 * n,)), dma((2 * n,)), dma((2,)), dma((2,)),
        dma((BANDS, n - 1)), dma((BANDS, n - 1)), dma((2 * n,)), dma((2 * n,)), dma((BANDS + 1,)), dma((BANDS + 1,)),
    ]
    return pl.pallas_call(
        kernel,
        out_shape=jax.ShapeDtypeStruct(scene.shape, F32),
        in_specs=[hbm] * 8,
        out_specs=vmem,
        scratch_shapes=scratch,
        compiler_params=pltpu.CompilerParams(
            collective_id=0, has_side_effects=True, vmem_limit_bytes=60 * 2**20
        ),
    )(
        scene,
        kernels_h.transpose(0, 2, 1, 3),
        kernels_v.transpose(0, 2, 1, 3),
        coeffs,
        observed,
        good_pixels,
        coverage.transpose(1, 0),
        offsets,
    )


def solution(mesh):
    in_specs = (
        P(None, "epoch", "tile"),
        P("epoch", None, None, None),
        P("epoch", None, None, None),
        P("epoch", None, None, "tile"),
        P("epoch", None, None, "tile"),
        P("epoch", None, "tile"),
        P("epoch", "tile"),
        P("epoch", "tile", None),
    )
    out_specs = P(None, "epoch", "tile")
    return jax.shard_map(
        per_device, mesh=mesh, in_specs=in_specs, out_specs=out_specs, check_vma=False
    )
```

```python
import jax
import jax.numpy as jnp
from jax import lax
from jax.experimental import pallas as pl
from jax.experimental.pallas import tpu as pltpu
from jax.sharding import PartitionSpec as P

BANDS, NBASIS, TAPS = 2, 5, 21
LOCAL = 2
ROWS, W, TILES = 256, 128, 8
BLOCK = 64
EDGE = 18
STEP = 2 * EDGE + 1
PAD = 32
REACH = 10
NX, NZ, NC = 4, 4, 2
F32, BF16 = jnp.float32, jnp.bfloat16
MESH = pl.DeviceIdType.MESH


def split2(value):
    hi = value.astype(BF16)
    return hi, (value - hi.astype(F32)).astype(BF16)


def mm(a, b):
    return jnp.dot(a, b, preferred_element_type=F32)


def prepare_taps(taps_in, taps):
    taps[...] = jnp.zeros_like(taps)
    lane = lax.broadcasted_iota(jnp.int32, (8, W), 1)
    for e in range(LOCAL):
        for b in range(BANDS):
            taps[0, e, b, 0:NBASIS, 0:TAPS] = taps_in[e, :, b, :]

    def step(i, carry):
        row = taps[0, i // BANDS, i % BANDS]
        back = jnp.zeros((8, W), F32)
        for a in range(TAPS):
            back = jnp.where(lane == TAPS - 1 - a, row[:, a : a + 1], back)
        taps[1, i // BANDS, i % BANDS] = back
        return carry

    lax.fori_loop(0, LOCAL * BANDS, step, 0)


def build_bands(offsets, th, tv, hf, hs, hb, vf, vb):
    row = lax.broadcasted_iota(jnp.int32, (W, W), 0)
    lane = lax.broadcasted_iota(jnp.int32, (W, W), 1)
    near = jnp.abs(row - lane) < W // 2

    def shifted(taps, flipped, e, b, k, shift, rows):
        base = jnp.broadcast_to(taps[flipped, e, b, pl.ds(k, 1), :], (8, W))
        for bit in (1, 2, 4):
            base = jnp.where((row[0:8] & bit) != 0, pltpu.roll(base, bit, axis=1), base)
        base = pltpu.roll(base, shift, axis=1)
        return jnp.concatenate([base] + [pltpu.roll(base, g, axis=1) for g in range(8, rows, 8)], axis=0)

    def circulant(taps, flipped, e, b, k, shift):
        full = shifted(taps, flipped, e, b, k, shift, W)
        return split2(jnp.where(near, full, 0.0)), split2(jnp.where(near, 0.0, full))

    def step(i, carry):
        b, k = i // NBASIS, i % NBASIS
        for e in range(LOCAL):
            dy, dx = offsets[e, 0, 0], offsets[e, 0, 1]
            cols = slice(e * W, (e + 1) * W)
            main, edge = circulant(th, 1, e, b, k, W - REACH - dx)
            for part in range(2):
                hf[part, b, k, :, cols] = main[part]
            hi, lo = edge[0].astype(F32), edge[1].astype(F32)
            mixed = hi + pltpu.roll(hi, STEP, axis=0) + pltpu.roll(lo, 2 * STEP, axis=0)
            hs[b, k, :, cols] = mixed.astype(BF16)
            main, edge = circulant(th, 0, e, b, k, W - REACH + dx)
            for part in range(2):
                hb[part, b, e, k, :, 0:W] = main[part]
                hb[part, b, e, k, :, W : 2 * W] = edge[part]
            for ref, flipped, shift in ((vf, 0, PAD - REACH + dy), (vb, 1, PAD - REACH - dy)):
                parts = split2(shifted(tv, flipped, e, b, k, shift, BLOCK))
                for part in range(2):
                    ref[part, b, e, k] = parts[part]
        return carry

    lax.fori_loop(0, BANDS * NBASIS, step, 0)


def blocks(parts):
    zero = jnp.zeros((PAD, W), BF16)
    columns = []
    for first in range(0, ROWS, BLOCK):
        rows = []
        for part in parts:
            inner = part[max(first - PAD, 0) : min(first + BLOCK + PAD, ROWS)]
            rows += [zero] * (first == 0) + [inner] + [zero] * (first + BLOCK == ROWS)
        columns.append(jnp.concatenate(rows, axis=0))
    return jnp.concatenate(columns, axis=1)


def side(value):
    return jnp.concatenate([value[i : i + BLOCK] for i in range(0, ROWS, BLOCK)], axis=1)


def upright(value):
    return jnp.concatenate([value[:, i : i + W] for i in range(0, value.shape[1], W)], axis=0)


def vertical(taps, parts):
    tall = mm(jnp.concatenate([jnp.concatenate([t, t], axis=1) for t in taps], axis=0), blocks(parts))
    return tall[0:BLOCK] + tall[BLOCK : 2 * BLOCK]


def packed_parts(value, lane, b):
    if b == 1:
        value = pltpu.roll(value, W // 2, axis=1)
    value = jnp.where((lane < EDGE) | (lane >= W - EDGE), value, 0.0)
    hi = value.astype(BF16).astype(F32)
    mixed = hi + pltpu.roll(value - hi, STEP, axis=1) + pltpu.roll(hi, 2 * STEP, axis=1)
    return mixed.astype(BF16)


def mm3(a, b):
    return mm(a[0], b[0]) + mm(a[1], b[0]) + mm(a[0], b[1])


def both(ref, *index):
    return ref[(0,) + index], ref[(1,) + index]


def epoch_terms(b, e, coverage, cv, ov, gv, vf, vb, am, pm):
    model = jnp.zeros((BLOCK, ROWS // BLOCK * W), F32)
    for k in range(NBASIS):
        down = vertical(both(vf, b, e, k), both(am, b, e, k))
        model = model + side(cv[e, k]).astype(F32) * down
    weight = (side(gv[e]) * coverage[0, e]).astype(F32)
    residual = weight * (model - side(ov[e, b]).astype(F32))
    for k in range(NBASIS):
        q = split2(upright(side(cv[e, k]).astype(F32) * residual))
        for part, p in enumerate(split2(vertical(both(vb, b, e, k), q))):
            pm[part, e * NBASIS + k] = upright(p)


def right_lanes(shape):
    return (lax.broadcasted_iota(jnp.int32, shape, len(shape) - 1) // (W // 4)) % 2 == 0


def fold(value, to_right):
    axis = value.ndim - 1
    below = pltpu.roll(value, 4, axis=axis - 1)
    below = pltpu.roll(below, W // 4 if to_right else 3 * W // 4, axis=axis)
    mixed = jnp.where(right_lanes(value.shape) == to_right, value, below)
    return mixed[..., 0:4, :]


def unfold(value, to_right):
    return pltpu.roll(value, 3 * W // 4 if to_right else W // 4, axis=value.ndim - 1)


def kernel(
    scene, kh, kv, coeffs, observed, good, coverage_in, offsets_in, out,
    field, packed_right, packed_left, sides, left, right, grad, from_core, half, from_e, half_right, half_left, from_left, from_right,
    khv, kvv, cv, ov, gv, coverage, offsets, th, tv, hf, hs, hb, vf, vb, am, pm, beside,
    local_sem, es, er, ss, sr, cs, cr, es2, er2, ss2, sr2, cs2, cr2,
):
    t, me = lax.axis_index("tile"), lax.axis_index("epoch")
    x, z, c = me // (NZ * NC), (me // NC) % NZ, me % NC

    def at(tile, xx, zz, cc):
        return {"tile": tile, "epoch": (xx * NZ + zz) * NC + cc}

    def remote(src, dst, ssem, rsem, where):
        return pltpu.make_async_remote_copy(
            src_ref=src, dst_ref=dst, send_sem=ssem, recv_sem=rsem, device_id=where, device_id_type=MESH
        )

    def signal(where):
        pl.semaphore_signal(barrier, inc=1, device_id=where, device_id_type=MESH)

    spots = [((x + i) % NX, (z + j) % NZ) for i in (2, 1, 3, 0) for j in (2, 1, 3, 0)]
    near = NX * NZ - 1
    has_left, has_right = t > 0, t < TILES - 1

    barrier = pltpu.get_barrier_semaphore()
    own = pltpu.make_async_copy(scene, field.at[:, x, z, c], local_sem.at[0])
    own.start()

    @pl.when(has_right)
    def _():
        for xx, zz in spots:
            signal(at(t + 1, xx, zz, c))

    @pl.when(has_left)
    def _():
        for xx, zz in spots:
            signal(at(t - 1, xx, zz, c))

    for xx, zz in spots[:near]:
        signal(at(t, xx, zz, c))
    signal(at(t, x, z, 1 - c))

    small = [
        pltpu.make_async_copy(kh, khv, local_sem.at[1]),
        pltpu.make_async_copy(kv, kvv, local_sem.at[2]),
        pltpu.make_async_copy(coverage_in, coverage, local_sem.at[3]),
        pltpu.make_async_copy(offsets_in, offsets, local_sem.at[4]),
    ]
    loads = [
        pltpu.make_async_copy(coeffs, cv, local_sem.at[5]),
        pltpu.make_async_copy(observed, ov, local_sem.at[6]),
        pltpu.make_async_copy(good, gv, local_sem.at[7]),
    ]
    for load in small + loads:
        load.start()
    own.wait()
    lane = lax.broadcasted_iota(jnp.int32, (8, W), 1)
    outer = (lane < W // 4) | (lane >= 3 * W // 4)
    turned = pltpu.roll(field[1, x, z, c], W // 2, axis=1)
    packed = jnp.where(outer, field[0, x, z, c], turned)
    packed_right[...] = fold(packed, True)
    packed_left[...] = fold(packed, False)
    for load in small:
        load.wait()
    prepare_taps(khv, th)
    prepare_taps(kvv, tv)
    count = near + 1 + len(spots) * (has_left.astype(jnp.int32) + has_right.astype(jnp.int32))
    pl.semaphore_wait(barrier, count)

    mine = field.at[:, x, z, c]
    mains = [remote(mine, mine, es.at[d], er.at[d], at(t, *spots[d], c)) for d in range(near)]
    n = len(spots)
    slot = x * NZ + z
    to_right = [remote(packed_left, left.at[slot], ss.at[d], sr.at[d], at(t + 1, *spots[d], c)) for d in range(n)]
    to_left = [remote(packed_right, right.at[slot], ss.at[n + d], sr.at[n + d], at(t - 1, *spots[d], c)) for d in range(n)]

    @pl.when(has_right)
    def _():
        for copy in to_right:
            copy.start()

    @pl.when(has_left)
    def _():
        for copy in to_left:
            copy.start()

    for copy in mains:
        copy.start()

    build_bands(offsets, th, tv, hf, hs, hb, vf, vb)
    for copy in mains:
        copy.wait_recv()
    rows = field.at[:, :, :, c]
    swap = remote(rows, rows, cs.at[0], cr.at[0], at(t, x, z, 1 - c))
    swap.start()
    for load in loads:
        load.wait()

    @pl.when(has_left)
    def _():
        for copy in to_right:
            copy.wait_recv()

    @pl.when(has_right)
    def _():
        for copy in to_left:
            copy.wait_recv()

    low = jnp.where(has_right, right[...], 0.0)
    high = jnp.where(has_left, left[...], 0.0)
    mask = right_lanes((n, 4, W))
    sides[:, :, c, 0:4] = jnp.where(mask, low, high).reshape(NX, NZ, 4, W)
    sides[:, :, c, 4:8] = jnp.where(mask, unfold(low, True), unfold(high, False)).reshape(NX, NZ, 4, W)
    rows = sides.at[:, :, c]
    swap_sides = remote(rows, rows, cs.at[1], cr.at[1], at(t, x, z, 1 - c))
    swap_sides.start()

    swap.wait_recv()
    parts = [split2(field[b].reshape(ROWS, W)) for b in range(BANDS)]
    swap_sides.wait_recv()
    beyond = sides[...].reshape(ROWS, W)
    lane = lax.broadcasted_iota(jnp.int32, (ROWS, W), 1)
    for b in range(BANDS):
        hi, lo = parts[b]
        x_all = jnp.concatenate([hi, lo, hi, packed_parts(beyond, lane, b)], axis=1)
        for k in range(NBASIS):
            h_all = jnp.concatenate([hf[0, b, k], hf[0, b, k], hf[1, b, k], hs[b, k]], axis=0)
            a = split2(mm(x_all, h_all))
            for part in range(2):
                for e in range(LOCAL):
                    am[part, b, e, k] = a[part][:, e * W : (e + 1) * W]

    depth = LOCAL * NBASIS * W
    shape = grad.shape[1:]

    def across(b):
        h = [hb[part, b].reshape(depth, 2 * W) for part in range(2)]
        p = [jnp.concatenate([pm[part, i] for i in range(LOCAL * NBASIS)], axis=1) for part in range(2)]
        return mm3(p, h)

    def sum_copy(b):
        return remote(grad.at[b, :, :, 1 - c], from_core.at[b], cs2.at[b], cr2.at[b], at(t, x, z, 1 - c))

    def take_sum(b):
        sum_copy(b).wait_recv()
        half[b] = grad[b, :, :, c] + from_core[b]

    def mains_of(b):
        return [
            remote(half.at[b, spots[d][0], spots[d][1]], from_e.at[b, d], es2.at[b, d], er2.at[b, d], at(t, *spots[d], c))
            for d in range(near)
        ]

    mains0, mains1 = mains_of(0), mains_of(1)
    wide = lax.broadcasted_iota(jnp.int32, (ROWS, W), 1)
    wide = (wide < W // 4) | (wide >= 3 * W // 4)

    def band_step(b, carry):
        def epoch_step(e, carry):
            epoch_terms(b, e, coverage, cv, ov, gv, vf, vb, am, pm)

            @pl.when((b == 1) & (e == 1))
            def _():
                take_sum(0)
                for copy in mains0:
                    copy.start()

            return carry

        lax.fori_loop(0, LOCAL, epoch_step, 0)
        full = across(b)
        edge = full[:, W : 2 * W]

        @pl.when(b == 0)
        def _():
            grad[BANDS] = edge.reshape(shape)

        @pl.when(b == 1)
        def _():
            first = grad[BANDS].reshape(ROWS, W)
            grad[BANDS] = jnp.where(wide, first, pltpu.roll(edge, W // 2, axis=1)).reshape(shape)
            sum_copy(BANDS).start()

        grad[b] = full[:, 0:W].reshape(shape)
        sum_copy(b).start()
        return carry

    lax.fori_loop(0, BANDS, band_step, 0)
    take_sum(BANDS)
    strips = half[BANDS].reshape(n, 8, W)
    half_right[...] = fold(strips, True).reshape(NX, NZ, 4, W)
    half_left[...] = fold(strips, False).reshape(NX, NZ, 4, W)
    to_right2 = [
        remote(half_right.at[spots[d][0], spots[d][1]], from_left.at[slot], ss2.at[d], sr2.at[d], at(t + 1, *spots[d], c))
        for d in range(n)
    ]
    to_left2 = [
        remote(
            half_left.at[spots[d][0], spots[d][1]], from_right.at[slot], ss2.at[n + d], sr2.at[n + d], at(t - 1, *spots[d], c)
        )
        for d in range(n)
    ]

    @pl.when(has_right)
    def _():
        for copy in to_right2:
            copy.start()

    @pl.when(has_left)
    def _():
        for copy in to_left2:
            copy.start()

    take_sum(1)
    for copy in mains1:
        copy.start()

    for copy in mains + [swap, swap_sides] + [sum_copy(b) for b in range(BANDS + 1)] + mains0 + mains1:
        copy.wait_send()

    @pl.when(has_right)
    def _():
        for copy in to_right + to_right2:
            copy.wait_send()

    @pl.when(has_left)
    def _():
        for copy in to_left + to_left2:
            copy.wait_send()

    for copy in mains0 + mains1:
        copy.wait_recv()

    @pl.when(has_left)
    def _():
        for copy in to_right2:
            copy.wait_recv()

    @pl.when(has_right)
    def _():
        for copy in to_left2:
            copy.wait_recv()

    lane = lax.broadcasted_iota(jnp.int32, (8, W), 1)
    lower = jnp.where(has_left, jnp.sum(from_left[...], axis=0), 0.0)
    upper = jnp.where(has_right, jnp.sum(from_right[...], axis=0), 0.0)
    mask = right_lanes((4, W))
    beside[0:4] = jnp.where(mask, lower, upper)
    beside[4:8] = jnp.where(mask, unfold(lower, True), unfold(upper, False))
    for b in range(BANDS):
        add = beside[...] if b == 0 else pltpu.roll(beside[...], W // 2, axis=1)
        out[b] = half[b, x, z] + jnp.sum(from_e[b], axis=0) + jnp.where(outer, add, 0.0)


def per_device(scene, kernels_h, kernels_v, coeffs, observed, good_pixels, coverage, offsets):
    vmem = pl.BlockSpec(memory_space=pltpu.VMEM)
    hbm = pl.BlockSpec(memory_space=pl.ANY)
    tile = (8, W)
    dma = pltpu.SemaphoreType.DMA
    chips = (NX, NZ)
    n = NX * NZ
    scratch = [
        pltpu.VMEM((BANDS, *chips, NC) + tile, F32),
        pltpu.VMEM((4, W), F32),
        pltpu.VMEM((4, W), F32),
        pltpu.VMEM((*chips, NC) + tile, F32),
        pltpu.VMEM((n, 4, W), F32),
        pltpu.VMEM((n, 4, W), F32),
        pltpu.VMEM((BANDS + 1, *chips, NC) + tile, F32),
        pltpu.VMEM((BANDS + 1, *chips) + tile, F32),
        pltpu.VMEM((BANDS + 1, *chips) + tile, F32),
        pltpu.VMEM((BANDS, n - 1) + tile, F32),
        pltpu.VMEM((*chips, 4, W), F32),
        pltpu.VMEM((*chips, 4, W), F32),
        pltpu.VMEM((n, 4, W), F32),
        pltpu.VMEM((n, 4, W), F32),
        pltpu.VMEM((LOCAL, NBASIS, BANDS, TAPS), F32),
        pltpu.VMEM((LOCAL, NBASIS, BANDS, TAPS), F32),
        pltpu.VMEM(coeffs.shape, BF16),
        pltpu.VMEM(observed.shape, BF16),
        pltpu.VMEM(good_pixels.shape, jnp.int32),
        pltpu.SMEM((1, LOCAL), jnp.int32),
        pltpu.SMEM(offsets.shape, jnp.int32),
        pltpu.VMEM((2, LOCAL, BANDS, 8, W), F32),
        pltpu.VMEM((2, LOCAL, BANDS, 8, W), F32),
        pltpu.VMEM((2, BANDS, NBASIS, W, LOCAL * W), BF16),
        pltpu.VMEM((BANDS, NBASIS, W, LOCAL * W), BF16),
        pltpu.VMEM((2, BANDS, LOCAL, NBASIS, W, 2 * W), BF16),
        pltpu.VMEM((2, BANDS, LOCAL, NBASIS, BLOCK, W), BF16),
        pltpu.VMEM((2, BANDS, LOCAL, NBASIS, BLOCK, W), BF16),
        pltpu.VMEM((2, BANDS, LOCAL, NBASIS, ROWS, W), BF16),
        pltpu.VMEM((2, LOCAL * NBASIS, ROWS, W), BF16),
        pltpu.VMEM(tile, F32),
        dma((8,)),
        dma((n - 1,)), dma((n - 1,)), dma((2 * n,)), dma((2 * n,)), dma((2,)), dma((2,)),
        dma((BANDS, n - 1)), dma((BANDS, n - 1)), dma((2 * n,)), dma((2 * n,)), dma((BANDS + 1,)), dma((BANDS + 1,)),
    ]
    return pl.pallas_call(
        kernel,
        out_shape=jax.ShapeDtypeStruct(scene.shape, F32),
        in_specs=[hbm] * 8,
        out_specs=vmem,
        scratch_shapes=scratch,
        compiler_params=pltpu.CompilerParams(
            collective_id=0, has_side_effects=True, vmem_limit_bytes=60 * 2**20
        ),
    )(
        scene,
        kernels_h.transpose(0, 2, 1, 3),
        kernels_v.transpose(0, 2, 1, 3),
        coeffs,
        observed,
        good_pixels,
        coverage.transpose(1, 0),
        offsets,
    )


def solution(mesh):
    in_specs = (
        P(None, "epoch", "tile"),
        P("epoch", None, None, None),
        P("epoch", None, None, None),
        P("epoch", None, None, "tile"),
        P("epoch", None, None, "tile"),
        P("epoch", None, "tile"),
        P("epoch", "tile"),
        P("epoch", "tile", None),
    )
    out_specs = P(None, "epoch", "tile")
    return jax.shard_map(
        per_device, mesh=mesh, in_specs=in_specs, out_specs=out_specs, check_vma=False
    )
```

```python
import jax
import jax.numpy as jnp
from jax import lax
from jax.experimental import pallas as pl
from jax.experimental.pallas import tpu as pltpu
from jax.sharding import PartitionSpec as P

BANDS, NBASIS, TAPS = 2, 5, 21
LOCAL = 2
ROWS, W, TILES = 256, 128, 8
BLOCK = 64
AHEAD = 4
EDGE = 18
STEP = 2 * EDGE + 1
PAD = 32
REACH = 10
NX, NZ, NC = 4, 4, 2
F32, BF16 = jnp.float32, jnp.bfloat16
MESH = pl.DeviceIdType.MESH


def split2(value):
    hi = value.astype(BF16)
    return hi, (value - hi.astype(F32)).astype(BF16)


def mm(a, b):
    return jnp.dot(a, b, preferred_element_type=F32)


def prepare_taps(taps_in, taps):
    taps[...] = jnp.zeros_like(taps)
    lane = lax.broadcasted_iota(jnp.int32, (8, W), 1)
    for e in range(LOCAL):
        for b in range(BANDS):
            taps[0, e, b, 0:NBASIS, 0:TAPS] = taps_in[e, :, b, :]

    def step(i, carry):
        row = taps[0, i // BANDS, i % BANDS]
        back = jnp.zeros((8, W), F32)
        for a in range(TAPS):
            back = jnp.where(lane == TAPS - 1 - a, row[:, a : a + 1], back)
        taps[1, i // BANDS, i % BANDS] = back
        return carry

    lax.fori_loop(0, LOCAL * BANDS, step, 0)


def build_bands(lo, hi, offsets, th, tv, hf, hs, hb, vf, vb):
    row = lax.broadcasted_iota(jnp.int32, (W, W), 0)
    lane = lax.broadcasted_iota(jnp.int32, (W, W), 1)
    near = jnp.abs(row - lane) < W // 2

    def shifted(taps, flipped, e, b, k, shift, rows):
        base = jnp.broadcast_to(taps[flipped, e, b, pl.ds(k, 1), :], (8, W))
        for bit in (1, 2, 4):
            base = jnp.where((row[0:8] & bit) != 0, pltpu.roll(base, bit, axis=1), base)
        base = pltpu.roll(base, shift, axis=1)
        return jnp.concatenate([base] + [pltpu.roll(base, g, axis=1) for g in range(8, rows, 8)], axis=0)

    def circulant(taps, flipped, e, b, k, shift):
        full = shifted(taps, flipped, e, b, k, shift, W)
        return split2(jnp.where(near, full, 0.0)), split2(jnp.where(near, 0.0, full))

    def step(i, carry):
        b, k = i // NBASIS, i % NBASIS
        for e in range(LOCAL):
            dy, dx = offsets[e, 0, 0], offsets[e, 0, 1]
            cols = slice(e * W, (e + 1) * W)
            main, edge = circulant(th, 1, e, b, k, W - REACH - dx)
            for part in range(2):
                hf[part, b, k, :, cols] = main[part]
            hi, lo = edge[0].astype(F32), edge[1].astype(F32)
            mixed = hi + pltpu.roll(hi, STEP, axis=0) + pltpu.roll(lo, 2 * STEP, axis=0)
            hs[b, k, :, cols] = mixed.astype(BF16)
            main, edge = circulant(th, 0, e, b, k, W - REACH + dx)
            for part in range(2):
                hb[part, b, e, k, :, 0:W] = main[part]
                hb[part, b, e, k, :, W : 2 * W] = edge[part]
            for ref, flipped, shift in ((vf, 0, PAD - REACH + dy), (vb, 1, PAD - REACH - dy)):
                parts = split2(shifted(tv, flipped, e, b, k, shift, BLOCK))
                for part in range(2):
                    ref[part, b, e, k] = parts[part]
        return carry

    lax.fori_loop(lo, hi, step, 0)


def blocks(parts):
    zero = jnp.zeros((PAD, W), BF16)
    columns = []
    for first in range(0, ROWS, BLOCK):
        rows = []
        for part in parts:
            inner = part[max(first - PAD, 0) : min(first + BLOCK + PAD, ROWS)]
            rows += [zero] * (first == 0) + [inner] + [zero] * (first + BLOCK == ROWS)
        columns.append(jnp.concatenate(rows, axis=0))
    return jnp.concatenate(columns, axis=1)


def side(value):
    return jnp.concatenate([value[i : i + BLOCK] for i in range(0, ROWS, BLOCK)], axis=1)


def upright(value):
    return jnp.concatenate([value[:, i : i + W] for i in range(0, value.shape[1], W)], axis=0)


def vertical(taps, parts):
    tall = mm(jnp.concatenate([jnp.concatenate([t, t], axis=1) for t in taps], axis=0), blocks(parts))
    return tall[0:BLOCK] + tall[BLOCK : 2 * BLOCK]


def packed_parts(value, lane, b):
    if b == 1:
        value = pltpu.roll(value, W // 2, axis=1)
    value = jnp.where((lane < EDGE) | (lane >= W - EDGE), value, 0.0)
    hi = value.astype(BF16).astype(F32)
    mixed = hi + pltpu.roll(value - hi, STEP, axis=1) + pltpu.roll(hi, 2 * STEP, axis=1)
    return mixed.astype(BF16)


def mm3(a, b):
    rows = a[0].shape[0]
    tall = mm(jnp.concatenate(a, axis=0), b[0])
    return tall[0:rows] + tall[rows:] + mm(a[0], b[1])


def both(ref, *index):
    return ref[(0,) + index], ref[(1,) + index]


def epoch_terms(b, e, coverage, cv, ov, gv, vf, vb, am, pm):
    model = jnp.zeros((BLOCK, ROWS // BLOCK * W), F32)
    for k in range(NBASIS):
        down = vertical(both(vf, b, e, k), both(am, b, e, k))
        model = model + side(cv[e, k]).astype(F32) * down
    weight = (side(gv[e]) * coverage[0, e]).astype(F32)
    residual = weight * (model - side(ov[e, b]).astype(F32))
    for k in range(NBASIS):
        q = split2(upright(side(cv[e, k]).astype(F32) * residual))
        for part, p in enumerate(split2(vertical(both(vb, b, e, k), q))):
            pm[part, e * NBASIS + k] = upright(p)


def right_lanes(shape):
    return (lax.broadcasted_iota(jnp.int32, shape, len(shape) - 1) // (W // 4)) % 2 == 0


def fold(value, to_right):
    axis = value.ndim - 1
    below = pltpu.roll(value, 4, axis=axis - 1)
    below = pltpu.roll(below, W // 4 if to_right else 3 * W // 4, axis=axis)
    mixed = jnp.where(right_lanes(value.shape) == to_right, value, below)
    return mixed[..., 0:4, :]


def unfold(value, to_right):
    return pltpu.roll(value, 3 * W // 4 if to_right else W // 4, axis=value.ndim - 1)


def kernel(
    scene, kh, kv, coeffs, observed, good, coverage_in, offsets_in, out,
    field, packed_right, packed_left, sides, left, right, grad, from_core, half, from_e, half_right, half_left, from_left, from_right,
    khv, kvv, cv, ov, gv, coverage, offsets, th, tv, hf, hs, hb, vf, vb, am, pm, beside,
    local_sem, es, er, ss, sr, cs, cr, es2, er2, ss2, sr2, cs2, cr2,
):
    t, me = lax.axis_index("tile"), lax.axis_index("epoch")
    x, z, c = me // (NZ * NC), (me // NC) % NZ, me % NC

    def at(tile, xx, zz, cc):
        return {"tile": tile, "epoch": (xx * NZ + zz) * NC + cc}

    def remote(src, dst, ssem, rsem, where):
        return pltpu.make_async_remote_copy(
            src_ref=src, dst_ref=dst, send_sem=ssem, recv_sem=rsem, device_id=where, device_id_type=MESH
        )

    def signal(where):
        pl.semaphore_signal(barrier, inc=1, device_id=where, device_id_type=MESH)

    spots = [((x + i) % NX, (z + j) % NZ) for i in (2, 1, 3, 0) for j in (2, 1, 3, 0)]
    near = NX * NZ - 1
    has_left, has_right = t > 0, t < TILES - 1

    barrier = pltpu.get_barrier_semaphore()
    own = pltpu.make_async_copy(scene, field.at[:, x, z, c], local_sem.at[0])
    own.start()

    @pl.when(has_right)
    def _():
        for xx, zz in spots:
            signal(at(t + 1, xx, zz, c))

    @pl.when(has_left)
    def _():
        for xx, zz in spots:
            signal(at(t - 1, xx, zz, c))

    for xx, zz in spots[:near]:
        signal(at(t, xx, zz, c))
    signal(at(t, x, z, 1 - c))

    small = [
        pltpu.make_async_copy(kh, khv, local_sem.at[1]),
        pltpu.make_async_copy(kv, kvv, local_sem.at[2]),
        pltpu.make_async_copy(coverage_in, coverage, local_sem.at[3]),
        pltpu.make_async_copy(offsets_in, offsets, local_sem.at[4]),
    ]
    loads = [
        pltpu.make_async_copy(coeffs, cv, local_sem.at[5]),
        pltpu.make_async_copy(observed, ov, local_sem.at[6]),
        pltpu.make_async_copy(good, gv, local_sem.at[7]),
    ]
    for load in small + loads:
        load.start()
    own.wait()
    lane = lax.broadcasted_iota(jnp.int32, (8, W), 1)
    outer = (lane < W // 4) | (lane >= 3 * W // 4)
    turned = pltpu.roll(field[1, x, z, c], W // 2, axis=1)
    packed = jnp.where(outer, field[0, x, z, c], turned)
    packed_right[...] = fold(packed, True)
    packed_left[...] = fold(packed, False)
    for load in small:
        load.wait()
    prepare_taps(khv, th)
    prepare_taps(kvv, tv)
    build_bands(0, AHEAD, offsets, th, tv, hf, hs, hb, vf, vb)
    count = near + 1 + len(spots) * (has_left.astype(jnp.int32) + has_right.astype(jnp.int32))
    pl.semaphore_wait(barrier, count)

    mine = field.at[:, x, z, c]
    mains = [remote(mine, mine, es.at[d], er.at[d], at(t, *spots[d], c)) for d in range(near)]
    n = len(spots)
    slot = x * NZ + z
    to_right = [remote(packed_left, left.at[slot], ss.at[d], sr.at[d], at(t + 1, *spots[d], c)) for d in range(n)]
    to_left = [remote(packed_right, right.at[slot], ss.at[n + d], sr.at[n + d], at(t - 1, *spots[d], c)) for d in range(n)]

    @pl.when(has_right)
    def _():
        for copy in to_right:
            copy.start()

    @pl.when(has_left)
    def _():
        for copy in to_left:
            copy.start()

    for copy in mains:
        copy.start()

    build_bands(AHEAD, BANDS * NBASIS, offsets, th, tv, hf, hs, hb, vf, vb)
    for copy in mains:
        copy.wait_recv()
    rows = field.at[:, :, :, c]
    swap = remote(rows, rows, cs.at[0], cr.at[0], at(t, x, z, 1 - c))
    swap.start()
    for load in loads:
        load.wait()

    @pl.when(has_left)
    def _():
        for copy in to_right:
            copy.wait_recv()

    @pl.when(has_right)
    def _():
        for copy in to_left:
            copy.wait_recv()

    low = jnp.where(has_right, right[...], 0.0)
    high = jnp.where(has_left, left[...], 0.0)
    mask = right_lanes((n, 4, W))
    sides[:, :, c, 0:4] = jnp.where(mask, low, high).reshape(NX, NZ, 4, W)
    sides[:, :, c, 4:8] = jnp.where(mask, unfold(low, True), unfold(high, False)).reshape(NX, NZ, 4, W)
    rows = sides.at[:, :, c]
    swap_sides = remote(rows, rows, cs.at[1], cr.at[1], at(t, x, z, 1 - c))
    swap_sides.start()

    swap.wait_recv()
    parts = [split2(field[b].reshape(ROWS, W)) for b in range(BANDS)]
    swap_sides.wait_recv()
    beyond = sides[...].reshape(ROWS, W)
    lane = lax.broadcasted_iota(jnp.int32, (ROWS, W), 1)
    for b in range(BANDS):
        hi, lo = parts[b]
        x_all = jnp.concatenate([hi, lo, hi, packed_parts(beyond, lane, b)], axis=1)
        for k in range(NBASIS):
            h_all = jnp.concatenate([hf[0, b, k], hf[0, b, k], hf[1, b, k], hs[b, k]], axis=0)
            a = split2(mm(x_all, h_all))
            for part in range(2):
                for e in range(LOCAL):
                    am[part, b, e, k] = a[part][:, e * W : (e + 1) * W]

    depth = LOCAL * NBASIS * W
    shape = grad.shape[1:]

    def across(b):
        h = [hb[part, b].reshape(depth, 2 * W) for part in range(2)]
        p = [jnp.concatenate([pm[part, i] for i in range(LOCAL * NBASIS)], axis=1) for part in range(2)]
        return mm3(p, h)

    def sum_copy(b):
        return remote(grad.at[b, :, :, 1 - c], from_core.at[b], cs2.at[b], cr2.at[b], at(t, x, z, 1 - c))

    def take_sum(b):
        sum_copy(b).wait_recv()
        half[b] = grad[b, :, :, c] + from_core[b]

    def mains_of(b):
        return [
            remote(half.at[b, spots[d][0], spots[d][1]], from_e.at[b, d], es2.at[b, d], er2.at[b, d], at(t, *spots[d], c))
            for d in range(near)
        ]

    mains0, mains1 = mains_of(0), mains_of(1)
    wide = lax.broadcasted_iota(jnp.int32, (ROWS, W), 1)
    wide = (wide < W // 4) | (wide >= 3 * W // 4)

    def band_step(b, carry):
        def epoch_step(e, carry):
            epoch_terms(b, e, coverage, cv, ov, gv, vf, vb, am, pm)

            @pl.when((b == 1) & (e == 1))
            def _():
                take_sum(0)
                for copy in mains0:
                    copy.start()

            return carry

        lax.fori_loop(0, LOCAL, epoch_step, 0)
        full = across(b)
        edge = full[:, W : 2 * W]

        @pl.when(b == 0)
        def _():
            grad[BANDS] = edge.reshape(shape)

        @pl.when(b == 1)
        def _():
            first = grad[BANDS].reshape(ROWS, W)
            grad[BANDS] = jnp.where(wide, first, pltpu.roll(edge, W // 2, axis=1)).reshape(shape)
            sum_copy(BANDS).start()

        grad[b] = full[:, 0:W].reshape(shape)
        sum_copy(b).start()
        return carry

    lax.fori_loop(0, BANDS, band_step, 0)
    take_sum(BANDS)
    strips = half[BANDS].reshape(n, 8, W)
    half_right[...] = fold(strips, True).reshape(NX, NZ, 4, W)
    half_left[...] = fold(strips, False).reshape(NX, NZ, 4, W)
    to_right2 = [
        remote(half_right.at[spots[d][0], spots[d][1]], from_left.at[slot], ss2.at[d], sr2.at[d], at(t + 1, *spots[d], c))
        for d in range(n)
    ]
    to_left2 = [
        remote(
            half_left.at[spots[d][0], spots[d][1]], from_right.at[slot], ss2.at[n + d], sr2.at[n + d], at(t - 1, *spots[d], c)
        )
        for d in range(n)
    ]

    @pl.when(has_right)
    def _():
        for copy in to_right2:
            copy.start()

    @pl.when(has_left)
    def _():
        for copy in to_left2:
            copy.start()

    take_sum(1)
    for copy in mains1:
        copy.start()

    for copy in mains + [swap, swap_sides] + [sum_copy(b) for b in range(BANDS + 1)] + mains0 + mains1:
        copy.wait_send()

    @pl.when(has_right)
    def _():
        for copy in to_right + to_right2:
            copy.wait_send()

    @pl.when(has_left)
    def _():
        for copy in to_left + to_left2:
            copy.wait_send()

    for copy in mains0 + mains1:
        copy.wait_recv()

    @pl.when(has_left)
    def _():
        for copy in to_right2:
            copy.wait_recv()

    @pl.when(has_right)
    def _():
        for copy in to_left2:
            copy.wait_recv()

    lane = lax.broadcasted_iota(jnp.int32, (8, W), 1)
    lower = jnp.where(has_left, jnp.sum(from_left[...], axis=0), 0.0)
    upper = jnp.where(has_right, jnp.sum(from_right[...], axis=0), 0.0)
    mask = right_lanes((4, W))
    beside[0:4] = jnp.where(mask, lower, upper)
    beside[4:8] = jnp.where(mask, unfold(lower, True), unfold(upper, False))
    for b in range(BANDS):
        add = beside[...] if b == 0 else pltpu.roll(beside[...], W // 2, axis=1)
        out[b] = half[b, x, z] + jnp.sum(from_e[b], axis=0) + jnp.where(outer, add, 0.0)


def per_device(scene, kernels_h, kernels_v, coeffs, observed, good_pixels, coverage, offsets):
    vmem = pl.BlockSpec(memory_space=pltpu.VMEM)
    hbm = pl.BlockSpec(memory_space=pl.ANY)
    tile = (8, W)
    dma = pltpu.SemaphoreType.DMA
    chips = (NX, NZ)
    n = NX * NZ
    scratch = [
        pltpu.VMEM((BANDS, *chips, NC) + tile, F32),
        pltpu.VMEM((4, W), F32),
        pltpu.VMEM((4, W), F32),
        pltpu.VMEM((*chips, NC) + tile, F32),
        pltpu.VMEM((n, 4, W), F32),
        pltpu.VMEM((n, 4, W), F32),
        pltpu.VMEM((BANDS + 1, *chips, NC) + tile, F32),
        pltpu.VMEM((BANDS + 1, *chips) + tile, F32),
        pltpu.VMEM((BANDS + 1, *chips) + tile, F32),
        pltpu.VMEM((BANDS, n - 1) + tile, F32),
        pltpu.VMEM((*chips, 4, W), F32),
        pltpu.VMEM((*chips, 4, W), F32),
        pltpu.VMEM((n, 4, W), F32),
        pltpu.VMEM((n, 4, W), F32),
        pltpu.VMEM((LOCAL, NBASIS, BANDS, TAPS), F32),
        pltpu.VMEM((LOCAL, NBASIS, BANDS, TAPS), F32),
        pltpu.VMEM(coeffs.shape, BF16),
        pltpu.VMEM(observed.shape, BF16),
        pltpu.VMEM(good_pixels.shape, jnp.int32),
        pltpu.SMEM((1, LOCAL), jnp.int32),
        pltpu.SMEM(offsets.shape, jnp.int32),
        pltpu.VMEM((2, LOCAL, BANDS, 8, W), F32),
        pltpu.VMEM((2, LOCAL, BANDS, 8, W), F32),
        pltpu.VMEM((2, BANDS, NBASIS, W, LOCAL * W), BF16),
        pltpu.VMEM((BANDS, NBASIS, W, LOCAL * W), BF16),
        pltpu.VMEM((2, BANDS, LOCAL, NBASIS, W, 2 * W), BF16),
        pltpu.VMEM((2, BANDS, LOCAL, NBASIS, BLOCK, W), BF16),
        pltpu.VMEM((2, BANDS, LOCAL, NBASIS, BLOCK, W), BF16),
        pltpu.VMEM((2, BANDS, LOCAL, NBASIS, ROWS, W), BF16),
        pltpu.VMEM((2, LOCAL * NBASIS, ROWS, W), BF16),
        pltpu.VMEM(tile, F32),
        dma((8,)),
        dma((n - 1,)), dma((n - 1,)), dma((2 * n,)), dma((2 * n,)), dma((2,)), dma((2,)),
        dma((BANDS, n - 1)), dma((BANDS, n - 1)), dma((2 * n,)), dma((2 * n,)), dma((BANDS + 1,)), dma((BANDS + 1,)),
    ]
    return pl.pallas_call(
        kernel,
        out_shape=jax.ShapeDtypeStruct(scene.shape, F32),
        in_specs=[hbm] * 8,
        out_specs=vmem,
        scratch_shapes=scratch,
        compiler_params=pltpu.CompilerParams(
            collective_id=0, has_side_effects=True, vmem_limit_bytes=60 * 2**20
        ),
    )(
        scene,
        kernels_h.transpose(0, 2, 1, 3),
        kernels_v.transpose(0, 2, 1, 3),
        coeffs,
        observed,
        good_pixels,
        coverage.transpose(1, 0),
        offsets,
    )


def solution(mesh):
    in_specs = (
        P(None, "epoch", "tile"),
        P("epoch", None, None, None),
        P("epoch", None, None, None),
        P("epoch", None, None, "tile"),
        P("epoch", None, None, "tile"),
        P("epoch", None, "tile"),
        P("epoch", "tile"),
        P("epoch", "tile", None),
    )
    out_specs = P(None, "epoch", "tile")
    return jax.shard_map(
        per_device, mesh=mesh, in_specs=in_specs, out_specs=out_specs, check_vma=False
    )
```
